256 devices in a mesh: dp: 32 (over y, z), tensor: 8 (over x, core).
Axes of the slice: x: 4, y: 4, z: 8, core: 2. Of those that a mesh axis runs over, the one named last changes fastest.
Arguments:
- gradient: bfloat16 [32, 4096, 4096], P('dp', None, 'tensor'), may hold values from -6 to 6
- error: bfloat16 [32, 4096, 4096], P('dp', None, 'tensor'), may hold values from -4 to 4
- q_prev: float32 [4096, 64], P('tensor'), may hold values from -0.09375 to 0.09375
Outputs:
- q_new: float32 [4096, 64], P('tensor')
- new_error: bfloat16 [32, 4096, 4096], P('dp', None, 'tensor')
The draws below stay inside these ranges and needn't reach their ends.
All inputs are finite; a program needn't handle non-finite values.
Results may differ from the reference program's by a relative error of at most 0.001.
Values sent between devices are 32-bit elements; how exact they have to be, the bound alone decides.
A program may use at most 64 MiB of HBM per device.

```python
import jax
import jax.numpy as jnp
from jax import lax

N = 4096
RANK = 64
ITERS = 2
N_DP = 32


def shard_levels(own_key, shape, cuts, smallest, high):
    loudness, own = 1.0, jax.random.fold_in(own_key, 6)
    for dim, parts in cuts:
        heights = jnp.exp(jax.random.uniform(jax.random.fold_in(own, dim), (parts,), jnp.float32, smallest / len(cuts), high / len(cuts)))
        loudness = loudness * jnp.repeat(heights, shape[dim] // parts).reshape([-1 if axis == dim else 1 for axis in range(len(shape))])
    return loudness


def gaussian(stream_key, dims, scale, limit, cuts=(), kind=jnp.bfloat16):
    loudness = shard_levels(stream_key, dims, cuts, -0.22, 0.18) if cuts else 1.0
    result = jax.random.normal(stream_key, dims, jnp.float32) * scale * loudness
    return jnp.minimum(jnp.maximum(result, -limit), limit).astype(kind)


def setup_inputs(seed: int = 0) -> dict:
    key_of = jax.random.split(jax.random.key(seed), 4)
    return {
        "gradient": gaussian(key_of[0], (N_DP, N, N), 1.0, 6.0, ((0, 32), (2, 8))),
        "error": gaussian(key_of[1], (N_DP, N, N), 0.5, 4.0, ((0, 32), (2, 8))),
        "q_prev": gaussian(key_of[2], (N, RANK), N ** -0.5, 0.09375, ((0, 8),), jnp.float32),
    }


HIGH = lax.Precision.HIGHEST

def merged_of(gradient, error, index):
    return gradient[index].astype(jnp.float32) + error[index].astype(jnp.float32)

def reference(gradient, error, q_prev):
    inverse = 1.0 / N_DP
    replicas = jnp.arange(N_DP, dtype=jnp.int32)
    q_current = q_prev
    p_hat = jnp.zeros((N, RANK), jnp.float32)
    for sweep in range(ITERS):

        def add_left(total, index):
            return (total + jnp.dot(merged_of(gradient, error, index), q_current, precision=HIGH), None)
        p_summed, unused = lax.scan(add_left, jnp.zeros((N, RANK), jnp.float32), replicas)
        p_summed = p_summed * inverse
        gram_matrix = jnp.dot(p_summed.T, p_summed, precision=HIGH)
        factor = jnp.linalg.cholesky(gram_matrix)
        p_hat = lax.linalg.triangular_solve(factor, p_summed, left_side=False, lower=True, transpose_a=True)

        def add_right(total, index):
            return (total + jnp.dot(merged_of(gradient, error, index).T, p_hat, precision=HIGH), None)
        q_summed, unused = lax.scan(add_right, jnp.zeros((N, RANK), jnp.float32), replicas)
        q_current = q_summed * inverse
    approx = jnp.dot(p_hat, q_current.T, precision=HIGH)

    def new_block(index):
        return (merged_of(gradient, error, index) - approx).astype(jnp.bfloat16)
    new_error = lax.map(new_block, replicas)
    return (q_current, new_error)
```

```python
import functools

import jax
import jax.numpy as jnp
from jax import lax
from jax.experimental import pallas as pl
from jax.experimental.pallas import tpu as pltpu
from jax.sharding import PartitionSpec as P

N = 4096
RANK = 64
ITERS = 2
NX, NY, NZ = 4, 4, 8
N_DP = NY * NZ
N_T = 2 * NX
COLS = N // N_T
CHUNK = N // N_T
LANES = 128
PIECES = 3
MESH = pl.DeviceIdType.MESH
HIGH = lax.Precision.HIGHEST
NT = (((1,), (1,)), ((), ()))


def ring_distance(step, size):
    return min(step % size, -step % size)


OFFSETS = sorted(
    [(dy, dz) for dy in range(NY) for dz in range(NZ) if dy or dz],
    key=lambda o: -(ring_distance(o[0], NY) + ring_distance(o[1], NZ)),
)


def split(value, pieces=PIECES):
    out = []
    for _ in range(pieces):
        piece = value.astype(jnp.bfloat16)
        out.append(piece)
        value = value - piece.astype(jnp.float32)
    return jnp.concatenate(out, axis=0)


def fold(value):
    total = value[0:RANK]
    for i in range(1, PIECES):
        total = total + value[i * RANK : (i + 1) * RANK]
    return total


def to_blocks(value):
    return jnp.concatenate(
        [value[:, l * LANES : (l + 1) * LANES].reshape(8, 8, LANES) for l in range(4)],
        axis=0,
    )


def from_blocks(value):
    return jnp.concatenate(
        [value[8 * l : 8 * l + 8].reshape(RANK, LANES) for l in range(4)], axis=1
    )


def eliminate(work, first, last):
    lane = lax.broadcasted_iota(jnp.int32, (RANK, 2 * RANK), 1)
    row = lax.broadcasted_iota(jnp.int32, (RANK, 1), 0)
    lane1 = lax.broadcasted_iota(jnp.int32, (1, 2 * RANK), 1)

    def step(j, carry):
        a = work[...]
        pivot_row = work[pl.ds(j, 1), :]
        pivot = jnp.sum(jnp.where(lane1 == j, pivot_row, 0.0), axis=1, keepdims=True)
        column = jnp.sum(jnp.where(lane == j, a, 0.0), axis=1, keepdims=True)
        column = jnp.where(row > j, column, 0.0)
        work[...] = a - column * (pivot_row / pivot)
        return carry

    lax.fori_loop(first, last, step, 0)


def inverse_factor(work):
    a = work[...]
    lane = lax.broadcasted_iota(jnp.int32, (RANK, 2 * RANK), 1)
    row = lax.broadcasted_iota(jnp.int32, (RANK, 2 * RANK), 0)
    diagonal = jnp.sum(jnp.where(lane == row, a, 0.0), axis=1, keepdims=True)
    return a[:, RANK:] / jnp.sqrt(diagonal)


def kernel(
    g_hbm, e_hbm, q_ref, q_out, new_out,
    g, e, qs, pp, sb, xs, xr, acc, yr, pg, qp, qr, qg, work, ph,
    load_sem, sib_send, sib_recv, x_send, x_recv, y_send, y_recv,
    ag_send, ag_recv, xg_send, xg_recv, sg_send, sg_recv,
    qr_send, qr_recv, qa_send, qa_recv,
):
    dp = lax.axis_index("dp")
    t = lax.axis_index("tensor")
    y, z = dp // NZ, dp % NZ
    x, c = t // 2, t % 2
    sibling = (dp, 2 * x + (1 - c))

    def dp_peer(o):
        return ((y + o[0]) % NY) * NZ + (z + o[1]) % NZ

    def x_at(d):
        return (x + d) % NX

    barrier = pltpu.get_barrier_semaphore()
    peers = [(dp_peer(o), t) for o in OFFSETS]
    everyone = peers + [sibling] + [(dp, 2 * x_at(d) + c) for d in (1, 2, 3)]
    for peer in everyone:
        pl.semaphore_signal(barrier, inc=1, device_id=peer, device_id_type=MESH)

    order = [2, 1, 3, 0]
    chunks = []
    for d in order:
        chunks += [2 * x_at(d) + (1 - c), 2 * x_at(d) + c]

    def rows_of(chunk):
        return pl.ds(pl.multiple_of(chunk * CHUNK, CHUNK), CHUNK)

    loads = []
    for i, chunk in enumerate(chunks):
        rows = rows_of(chunk)
        pair = []
        for k, (hbm, vmem) in enumerate(((g_hbm, g), (e_hbm, e))):
            copy = pltpu.make_async_copy(
                hbm.at[0, rows, :], vmem.at[rows, :], load_sem.at[i, k]
            )
            copy.start()
            pair.append(copy)
        loads.append(pair)

    qs[...] = split(q_ref[...])

    sends = []

    def send(src, dst, send_sem, recv_sem, device):
        copy = pltpu.make_async_remote_copy(
            src_ref=src,
            dst_ref=dst,
            send_sem=send_sem,
            recv_sem=recv_sem,
            device_id=device,
            device_id_type=MESH,
        )
        copy.start()
        return copy

    def wait_bytes(ref, sem):
        pltpu.make_async_copy(ref, ref, sem).wait()

    for it in range(ITERS):
        scale = 1.0 / N_DP

        def p_chunk(chunk):
            rows = rows_of(chunk)
            lhs = qs[...]
            a = lax.dot_general(lhs, g[rows, :], NT, preferred_element_type=jnp.float32)
            b = lax.dot_general(lhs, e[rows, :], NT, preferred_element_type=jnp.float32)
            return to_blocks(fold(a + b))

        def pass_on(d):
            wait_bytes(sb.at[it, d], sib_recv.at[it, d])
            total = xs[it, d] + sb[it, d]
            xs[it, d] = total
            if d:
                sends.append(
                    send(
                        xs.at[it, d],
                        xr.at[it, d - 1],
                        x_send.at[it, d - 1],
                        x_recv.at[it, d - 1],
                        (dp, 2 * x_at(d) + c),
                    )
                )

        for i, d in enumerate(order):
            if it == 0:
                loads[2 * i][0].wait()
                loads[2 * i][1].wait()
            pp[it, d] = p_chunk(chunks[2 * i])
            if it == 0 and i == 0:
                pl.semaphore_wait(barrier, len(everyone))
            sends.append(
                send(
                    pp.at[it, d],
                    sb.at[it, d],
                    sib_send.at[it, d],
                    sib_recv.at[it, d],
                    sibling,
                )
            )
            if it == 0:
                loads[2 * i + 1][0].wait()
                loads[2 * i + 1][1].wait()
            xs[it, d] = p_chunk(chunks[2 * i + 1])
            if i:
                pass_on(order[i - 1])
        pass_on(order[-1])

        total = xs[it, 0]
        for d in (1, 3, 2):
            wait_bytes(xr.at[it, d - 1], x_recv.at[it, d - 1])
            total = total + xr[it, d - 1]
        acc[it] = total * scale

        for k, peer in enumerate(peers):
            send(
                acc.at[it, peer[0]],
                yr.at[it, k],
                y_send.at[it],
                y_recv.at[it],
                peer,
            )
        own = acc[it, dp]
        wait_bytes(yr.at[it], y_recv.at[it])
        pg[it, t, dp] = own + jnp.sum(yr[it], axis=0)

        for peer in peers:
            send(
                pg.at[it, t, dp],
                pg.at[it, t, dp],
                ag_send.at[it],
                ag_recv.at[it],
                peer,
            )
        wait_bytes(yr.at[it], ag_recv.at[it])

        def share(d):
            slot = pg.at[it, 2 * x_at(-d) + c]
            return send(slot, slot, sg_send.at[it, d], sg_recv.at[it, d], sibling)

        for d in (2, 1, 3):
            sends.append(
                send(
                    pg.at[it, t],
                    pg.at[it, t],
                    xg_send.at[it, d - 1],
                    xg_recv.at[it, d - 1],
                    (dp, 2 * x_at(d) + c),
                )
            )
        sends.append(share(0))

        q_acc = jnp.zeros((RANK, COLS), jnp.float32)
        gram = jnp.zeros((PIECES * RANK, PIECES * RANK), jnp.float32)

        def q_chunk(chunk, q_acc, gram):
            rows = rows_of(chunk)
            lhs = split(from_blocks(pg[it, chunk]))
            a = jnp.dot(lhs, g[rows, :], preferred_element_type=jnp.float32)
            b = jnp.dot(lhs, e[rows, :], preferred_element_type=jnp.float32)
            more = lax.dot_general(lhs, lhs, NT, preferred_element_type=jnp.float32)
            return q_acc + fold(a + b), gram + more

        q_acc, gram = q_chunk(t, q_acc, gram)
        for d in (1, 3, 2):
            chunk = 2 * x_at(-d) + c
            wait_bytes(pg.at[it, chunk], xg_recv.at[it, d - 1])
            sends.append(share(d))
            q_acc, gram = q_chunk(chunk, q_acc, gram)
        for d in (0, 1, 3, 2):
            chunk = 2 * x_at(-d) + (1 - c)
            wait_bytes(pg.at[it, chunk], sg_recv.at[it, d])
            q_acc, gram = q_chunk(chunk, q_acc, gram)

        qp[it] = to_blocks(q_acc * scale)
        for k, peer in enumerate(peers):
            send(
                qp.at[it, peer[0]],
                qr.at[it, k],
                qr_send.at[it],
                qr_recv.at[it],
                peer,
            )

        square = jnp.zeros((RANK, RANK), jnp.float32)
        for i in range(PIECES):
            for j in range(PIECES):
                square = square + gram[
                    i * RANK : (i + 1) * RANK, j * RANK : (j + 1) * RANK
                ]
        row = lax.broadcasted_iota(jnp.int32, (RANK, RANK), 0)
        lane = lax.broadcasted_iota(jnp.int32, (RANK, RANK), 1)
        eye = jnp.where(row == lane, 1.0, 0.0)
        work[...] = jnp.concatenate([square, eye], axis=1)
        eliminate(work, 0, RANK // 2)

        wait_bytes(qr.at[it], qr_recv.at[it])
        qg[it, dp] = qp[it, dp] + jnp.sum(qr[it], axis=0)
        for peer in peers:
            send(
                qg.at[it, dp],
                qg.at[it, dp],
                qa_send.at[it],
                qa_recv.at[it],
                peer,
            )
        eliminate(work, RANK // 2, RANK)
        l_inverse = inverse_factor(work)

        if it == ITERS - 1:
            for chunk in range(N_T):
                p_t = from_blocks(pg[it, chunk])
                hat = jnp.dot(
                    l_inverse, p_t, precision=HIGH, preferred_element_type=jnp.float32
                )
                high = hat.astype(jnp.bfloat16).astype(jnp.float32)
                both = jnp.concatenate([high, hat - high], axis=0).T
                both = both.astype(jnp.bfloat16)
                ph[chunk * CHUNK : (chunk + 1) * CHUNK, :] = jnp.concatenate(
                    [both, both], axis=1
                )

        wait_bytes(qr.at[it], qa_recv.at[it])
        q_now = jnp.dot(
            l_inverse,
            from_blocks(qg[it]),
            precision=HIGH,
            preferred_element_type=jnp.float32,
        )
        if it < ITERS - 1:
            qs[...] = split(q_now)
        else:
            q_out[...] = q_now
            high = q_now.astype(jnp.bfloat16)
            low = (q_now - high.astype(jnp.float32)).astype(jnp.bfloat16)
            right = jnp.concatenate([high, high, low, low], axis=0)
            for chunk in range(N_T):
                rows = slice(chunk * CHUNK, (chunk + 1) * CHUNK)
                approx = jnp.dot(
                    ph[rows, :], right, preferred_element_type=jnp.float32
                )
                merged = g[rows, :].astype(jnp.float32) + e[rows, :].astype(jnp.float32)
                new_out[0, rows, :] = (merged - approx).astype(jnp.bfloat16)

    for copy in sends:
        copy.wait_send()
    for it in range(ITERS):
        for sem in (y_send, ag_send, qr_send, qa_send):
            wait_bytes(yr.at[it], sem.at[it])


def body(gradient, error, q_prev):
    f32, bf16 = jnp.float32, jnp.bfloat16
    blocks = (N_DP, 8, LANES)
    dma = pltpu.SemaphoreType.DMA
    vmem = pl.BlockSpec(memory_space=pltpu.VMEM)
    hbm = pl.BlockSpec(memory_space=pltpu.HBM)
    q_t, new_error = pl.pallas_call(
        kernel,
        out_shape=(
            jax.ShapeDtypeStruct((RANK, COLS), f32),
            jax.ShapeDtypeStruct((1, N, COLS), bf16),
        ),
        in_specs=[hbm, hbm, vmem],
        out_specs=(vmem, vmem),
        scratch_shapes=[
            pltpu.VMEM((N, COLS), bf16),
            pltpu.VMEM((N, COLS), bf16),
            pltpu.VMEM((PIECES * RANK, COLS), bf16),
            pltpu.VMEM((ITERS, NX, *blocks), f32),
            pltpu.VMEM((ITERS, NX, *blocks), f32),
            pltpu.VMEM((ITERS, NX, *blocks), f32),
            pltpu.VMEM((ITERS, NX - 1, *blocks), f32),
            pltpu.VMEM((ITERS, *blocks), f32),
            pltpu.VMEM((ITERS, N_DP - 1, 8, LANES), f32),
            pltpu.VMEM((ITERS, N_T, *blocks), f32),
            pltpu.VMEM((ITERS, *blocks), f32),
            pltpu.VMEM((ITERS, N_DP - 1, 8, LANES), f32),
            pltpu.VMEM((ITERS, *blocks), f32),
            pltpu.VMEM((RANK, 2 * RANK), f32),
            pltpu.VMEM((N, 4 * RANK), bf16),
            dma((N_T, 2)),
            dma((ITERS, NX)),
            dma((ITERS, NX)),
            dma((ITERS, NX - 1)),
            dma((ITERS, NX - 1)),
            dma((ITERS,)),
            dma((ITERS,)),
            dma((ITERS,)),
            dma((ITERS,)),
            dma((ITERS, NX - 1)),
            dma((ITERS, NX - 1)),
            dma((ITERS, NX)),
            dma((ITERS, NX)),
            dma((ITERS,)),
            dma((ITERS,)),
            dma((ITERS,)),
            dma((ITERS,)),
        ],
        compiler_params=pltpu.CompilerParams(
            collective_id=1, has_side_effects=True, vmem_limit_bytes=54 * 2**20
        ),
    )(gradient, error, q_prev.T)
    return q_t.T, new_error


def solution(mesh):
    return jax.shard_map(
        body,
        mesh=mesh,
        in_specs=(P("dp", None, "tensor"), P("dp", None, "tensor"), P("tensor", None)),
        out_specs=(P("tensor", None), P("dp", None, "tensor")),
        check_vma=False,
    )
```

```python
import functools

import jax
import jax.numpy as jnp
from jax import lax
from jax.experimental import pallas as pl
from jax.experimental.pallas import tpu as pltpu
from jax.sharding import PartitionSpec as P

N = 4096
RANK = 64
ITERS = 2
NX, NY, NZ = 4, 4, 8
N_DP = NY * NZ
N_T = 2 * NX
COLS = N // N_T
LANES = 128
PIECES = 3
MESH = pl.DeviceIdType.MESH
HIGH = lax.Precision.HIGHEST
NT = (((1,), (1,)), ((), ()))


def ring_distance(step, size):
    return min(step % size, -step % size)


def distance(o):
    return ring_distance(o[0], NY) + ring_distance(o[1], NZ)


OFFSETS = sorted(
    [(du, dz) for du in range(NY) for dz in range(NZ) if du or dz],
    key=lambda o: -distance(o),
)
FAR_FIRST = (4, 3, 5, 2, 6, 1, 7, 0)
NEAR_FIRST = FAR_FIRST[::-1]
GROUPS = 2 * NZ
ROWS = N // GROUPS


def split(value, pieces=PIECES):
    out = []
    for _ in range(pieces):
        piece = value.astype(jnp.bfloat16)
        out.append(piece)
        value = value - piece.astype(jnp.float32)
    return jnp.concatenate(out, axis=0)


def fold(value):
    total = value[0:RANK]
    for i in range(1, PIECES):
        total = total + value[i * RANK : (i + 1) * RANK]
    return total


def to_tiles(value):
    parts = [
        value[:, l * LANES : (l + 1) * LANES].reshape(8, 8, LANES)
        for l in range(value.shape[1] // LANES)
    ]
    return jnp.concatenate(parts, axis=0)


def from_tiles(value):
    parts = [
        value[8 * l : 8 * l + 8].reshape(RANK, LANES)
        for l in range(value.shape[0] // 8)
    ]
    return jnp.concatenate(parts, axis=1)


def eliminate(work, first, last):
    lane = lax.broadcasted_iota(jnp.int32, (RANK, 2 * RANK), 1)
    row = lax.broadcasted_iota(jnp.int32, (RANK, 1), 0)
    lane1 = lax.broadcasted_iota(jnp.int32, (1, 2 * RANK), 1)

    def step(j, carry):
        a = work[...]
        pivot_row = work[pl.ds(j, 1), :]
        pivot = jnp.sum(jnp.where(lane1 == j, pivot_row, 0.0), axis=1, keepdims=True)
        column = jnp.sum(jnp.where(lane == j, a, 0.0), axis=1, keepdims=True)
        column = jnp.where(row > j, column, 0.0)
        work[...] = a - column * (pivot_row / pivot)
        return carry

    lax.fori_loop(first, last, step, 0)


def inverse_factor(work):
    a = work[...]
    lane = lax.broadcasted_iota(jnp.int32, (RANK, 2 * RANK), 1)
    row = lax.broadcasted_iota(jnp.int32, (RANK, 2 * RANK), 0)
    diagonal = jnp.sum(jnp.where(lane == row, a, 0.0), axis=1, keepdims=True)
    return a[:, RANK:] / jnp.sqrt(diagonal)


def kernel(
    g_hbm, e_hbm, q_ref, q_out, new_out,
    g, e, qs, pp, sb, xs, xr, acc, yr, pg, qp, qr, qg, work, ph,
    load_sem, sib_send, sib_recv, x_send, x_recv, y_send, y_recv,
    ag_send, ag_recv, xg_send, xg_recv, sg_send, sg_recv,
    qr_send, qr_recv, qa_send, qa_recv,
):
    dp = lax.axis_index("dp")
    t = lax.axis_index("tensor")
    y, z = dp // NZ, dp % NZ
    x, c = t // 2, t % 2
    sibling = (dp, 2 * x + (1 - c))

    def device(y_at, z_at, x_at):
        return (y_at * NZ + z_at, 2 * x_at + c)

    def z_of(dz):
        return (z + dz) % NZ

    def line_place(z_at):
        odd = z_at % 2
        return x * (1 - odd) + y * odd

    def plane_place(z_at):
        odd = z_at % 2
        return y * (1 - odd) + x * odd

    def on_line(place, z_at):
        odd = z_at % 2
        return device(y * (1 - odd) + place * odd, z, place * (1 - odd) + x * odd)

    def on_plane(place, z_at, owner_z):
        odd = owner_z % 2
        return device(place * (1 - odd) + y * odd, z_at, x * (1 - odd) + place * odd)

    dp_peers = [device((y + o[0]) % NY, z_of(o[1]), x) for o in OFFSETS]
    others = [device(y, z_of(o[1]), (x + o[0]) % NX) for o in OFFSETS if o[0]]
    everyone = dp_peers + others + [sibling]

    def rows_of(core, z_at):
        return pl.ds(pl.multiple_of((core * NZ + z_at) * ROWS, ROWS), ROWS)

    loads = []
    for i, dz in enumerate(FAR_FIRST):
        for core in (1 - c, c):
            rows = rows_of(core, z_of(dz))
            pair = []
            for k, (hbm, vmem) in enumerate(((g_hbm, g), (e_hbm, e))):
                copy = pltpu.make_async_copy(
                    hbm.at[0, rows, :], vmem.at[rows, :], load_sem.at[len(loads), k]
                )
                copy.start()
                pair.append(copy)
            loads.append(pair)

    barrier = pltpu.get_barrier_semaphore()
    for peer in everyone:
        pl.semaphore_signal(barrier, inc=1, device_id=peer, device_id_type=MESH)

    qs[...] = split(q_ref[...])

    def send(src, dst, send_sem, recv_sem, target):
        pltpu.make_async_remote_copy(
            src_ref=src,
            dst_ref=dst,
            send_sem=send_sem,
            recv_sem=recv_sem,
            device_id=target,
            device_id_type=MESH,
        ).start()

    def wait_bytes(ref, sem):
        pltpu.make_async_copy(ref, ref, sem).wait()

    scale = 1.0 / N_DP
    for it in range(ITERS):

        def p_chunk(core, z_at):
            rows = rows_of(core, z_at)
            lhs = qs[...]
            a = lax.dot_general(lhs, g[rows, :], NT, preferred_element_type=jnp.float32)
            b = lax.dot_general(lhs, e[rows, :], NT, preferred_element_type=jnp.float32)
            return to_tiles(fold(a + b))

        def pass_along(dz):
            wait_bytes(sb.at[it, dz], sib_recv.at[it, dz])
            xs[it, dz] = xs[it, dz] + sb[it, dz]
            here = line_place(z_of(dz))
            for d in (2, 1, 3):
                place = (here + d) % NX
                send(
                    xs.at[it, dz, pl.ds(4 * place, 4)],
                    xr.at[it, dz, d - 1],
                    x_send.at[it],
                    x_recv.at[it, dz],
                    on_line(place, z_of(dz)),
                )

        for i, dz in enumerate(FAR_FIRST):
            if it == 0:
                for copy in loads[2 * i]:
                    copy.wait()
            pp[it, dz] = p_chunk(1 - c, z_of(dz))
            if it == 0 and i == 0:
                pl.semaphore_wait(barrier, len(everyone))
            send(
                pp.at[it, dz],
                sb.at[it, dz],
                sib_send.at[it],
                sib_recv.at[it, dz],
                sibling,
            )
            if it == 0:
                for copy in loads[2 * i + 1]:
                    copy.wait()
            xs[it, dz] = p_chunk(c, z_of(dz))
            if i:
                pass_along(FAR_FIRST[i - 1])
        pass_along(FAR_FIRST[-1])

        slot = 0
        for dz in FAR_FIRST:
            wait_bytes(xr.at[it, dz], x_recv.at[it, dz])
            total = xs[it, dz, pl.ds(4 * line_place(z_of(dz)), 4)]
            for d in (1, 2, 3):
                total = total + xr[it, dz, d - 1]
            acc[it, dz] = total * scale
            for du in (2, 1, 3, 0):
                if not (du or dz):
                    continue
                place = (plane_place(z_of(dz)) + du) % NY
                send(
                    acc.at[it, dz, place],
                    yr.at[it, slot],
                    y_send.at[it],
                    y_recv.at[it],
                    on_plane(place, z_of(dz), z_of(dz)),
                )
                slot += 1

        mine = 4 * line_place(z) + plane_place(z)
        own = acc[it, 0, plane_place(z)]
        wait_bytes(yr.at[it], y_recv.at[it])
        pg[it, c * NZ + z, mine] = own + jnp.sum(yr[it], axis=0)

        for du, dz in OFFSETS:
            tile = pg.at[it, c * NZ + z, mine]
            place = (plane_place(z) + du) % NY
            send(
                tile,
                tile,
                ag_send.at[it],
                ag_recv.at[it, dz],
                on_plane(place, z_of(dz), z),
            )

        for dz in NEAR_FIRST:
            z_at = z_of(-dz)
            here = line_place(z_at)
            tiles = pg.at[it, c * NZ + z_at, pl.ds(4 * here, 4)]
            if dz:
                wait_bytes(tiles, ag_recv.at[it, dz])
            else:
                wait_bytes(yr.at[it, pl.ds(0, 3)], ag_recv.at[it, dz])
            for d in (2, 1, 3):
                send(
                    tiles,
                    tiles,
                    xg_send.at[it],
                    xg_recv.at[it, dz],
                    on_line((here + d) % NX, z_at),
                )

        q_acc = jnp.zeros((RANK, COLS), jnp.float32)
        gram = jnp.zeros((PIECES * RANK, PIECES * RANK), jnp.float32)

        def q_chunk(core, z_at, q_acc, gram):
            rows = rows_of(core, z_at)
            lhs = split(from_tiles(pg[it, core * NZ + z_at]))
            a = jnp.dot(lhs, g[rows, :], preferred_element_type=jnp.float32)
            b = jnp.dot(lhs, e[rows, :], preferred_element_type=jnp.float32)
            more = lax.dot_general(lhs, lhs, NT, preferred_element_type=jnp.float32)
            return q_acc + fold(a + b), gram + more

        for dz in NEAR_FIRST:
            z_at = z_of(-dz)
            wait_bytes(xr.at[it, 0], xg_recv.at[it, dz])
            chunk = pg.at[it, c * NZ + z_at]
            send(chunk, chunk, sg_send.at[it], sg_recv.at[it, dz], sibling)
            q_acc, gram = q_chunk(c, z_at, q_acc, gram)
        for dz in NEAR_FIRST:
            z_at = z_of(-dz)
            wait_bytes(pg.at[it, (1 - c) * NZ + z_at], sg_recv.at[it, dz])
            q_acc, gram = q_chunk(1 - c, z_at, q_acc, gram)

        qp[it] = to_tiles(q_acc * scale)
        for k, peer in enumerate(dp_peers):
            send(
                qp.at[it, peer[0]],
                qr.at[it, k],
                qr_send.at[it],
                qr_recv.at[it],
                peer,
            )

        square = jnp.zeros((RANK, RANK), jnp.float32)
        for i in range(PIECES):
            for j in range(PIECES):
                square = square + gram[
                    i * RANK : (i + 1) * RANK, j * RANK : (j + 1) * RANK
                ]
        row = lax.broadcasted_iota(jnp.int32, (RANK, RANK), 0)
        lane = lax.broadcasted_iota(jnp.int32, (RANK, RANK), 1)
        eye = jnp.where(row == lane, 1.0, 0.0)
        work[...] = jnp.concatenate([square, eye], axis=1)
        eliminate(work, 0, RANK // 2)

        wait_bytes(qr.at[it], qr_recv.at[it])
        qg[it, dp] = qp[it, dp] + jnp.sum(qr[it], axis=0)
        for peer in dp_peers:
            send(
                qg.at[it, dp],
                qg.at[it, dp],
                qa_send.at[it],
                qa_recv.at[it],
                peer,
            )
        eliminate(work, RANK // 2, RANK)
        l_inverse = inverse_factor(work)

        if it == ITERS - 1:
            for i in range(GROUPS):
                hat = jnp.dot(
                    l_inverse,
                    from_tiles(pg[it, i]),
                    precision=HIGH,
                    preferred_element_type=jnp.float32,
                )
                high = hat.astype(jnp.bfloat16).astype(jnp.float32)
                both = jnp.concatenate([high, hat - high], axis=0).T
                both = both.astype(jnp.bfloat16)
                ph[i * ROWS : (i + 1) * ROWS, :] = jnp.concatenate([both, both], axis=1)

        wait_bytes(pp.at[it], sib_send.at[it])
        wait_bytes(xr.at[it], x_send.at[it])
        wait_bytes(yr.at[it], y_send.at[it])
        wait_bytes(yr.at[it], ag_send.at[it])
        wait_bytes(xr.at[it], xg_send.at[it])
        wait_bytes(pp.at[it], sg_send.at[it])
        wait_bytes(qr.at[it], qr_send.at[it])

        wait_bytes(qr.at[it], qa_recv.at[it])
        q_now = jnp.dot(
            l_inverse,
            from_tiles(qg[it]),
            precision=HIGH,
            preferred_element_type=jnp.float32,
        )
        if it < ITERS - 1:
            qs[...] = split(q_now)
        else:
            q_out[...] = q_now
            high = q_now.astype(jnp.bfloat16)
            low = (q_now - high.astype(jnp.float32)).astype(jnp.bfloat16)
            right = jnp.concatenate([high, high, low, low], axis=0)
            for i in range(N_T):
                rows = slice(i * COLS, (i + 1) * COLS)
                approx = jnp.dot(
                    ph[rows, :], right, preferred_element_type=jnp.float32
                )
                merged = g[rows, :].astype(jnp.float32) + e[rows, :].astype(jnp.float32)
                new_out[0, rows, :] = (merged - approx).astype(jnp.bfloat16)

    for it in range(ITERS):
        wait_bytes(qr.at[it], qa_send.at[it])


def body(gradient, error, q_prev):
    f32, bf16 = jnp.float32, jnp.bfloat16
    dma = pltpu.SemaphoreType.DMA
    vmem = pl.BlockSpec(memory_space=pltpu.VMEM)
    hbm = pl.BlockSpec(memory_space=pltpu.HBM)
    q_t, new_error = pl.pallas_call(
        kernel,
        out_shape=(
            jax.ShapeDtypeStruct((RANK, COLS), f32),
            jax.ShapeDtypeStruct((1, N, COLS), bf16),
        ),
        in_specs=[hbm, hbm, vmem],
        out_specs=(vmem, vmem),
        scratch_shapes=[
            pltpu.VMEM((N, COLS), bf16),
            pltpu.VMEM((N, COLS), bf16),
            pltpu.VMEM((PIECES * RANK, COLS), bf16),
            pltpu.VMEM((ITERS, NZ, 16, 8, LANES), f32),
            pltpu.VMEM((ITERS, NZ, 16, 8, LANES), f32),
            pltpu.VMEM((ITERS, NZ, 16, 8, LANES), f32),
            pltpu.VMEM((ITERS, NZ, 3, 4, 8, LANES), f32),
            pltpu.VMEM((ITERS, NZ, 4, 8, LANES), f32),
            pltpu.VMEM((ITERS, N_DP - 1, 8, LANES), f32),
            pltpu.VMEM((ITERS, GROUPS, 16, 8, LANES), f32),
            pltpu.VMEM((ITERS, N_DP, 8, LANES), f32),
            pltpu.VMEM((ITERS, N_DP - 1, 8, LANES), f32),
            pltpu.VMEM((ITERS, N_DP, 8, LANES), f32),
            pltpu.VMEM((RANK, 2 * RANK), f32),
            pltpu.VMEM((N, 4 * RANK), bf16),
            dma((GROUPS, 2)),
            dma((ITERS,)),
            dma((ITERS, NZ)),
            dma((ITERS,)),
            dma((ITERS, NZ)),
            dma((ITERS,)),
            dma((ITERS,)),
            dma((ITERS,)),
            dma((ITERS, NZ)),
            dma((ITERS,)),
            dma((ITERS, NZ)),
            dma((ITERS,)),
            dma((ITERS, NZ)),
            dma((ITERS,)),
            dma((ITERS,)),
            dma((ITERS,)),
            dma((ITERS,)),
        ],
        compiler_params=pltpu.CompilerParams(
            collective_id=1, has_side_effects=True, vmem_limit_bytes=48 * 2**20
        ),
    )(gradient, error, q_prev.T)
    return q_t.T, new_error


def solution(mesh):
    return jax.shard_map(
        body,
        mesh=mesh,
        in_specs=(P("dp", None, "tensor"), P("dp", None, "tensor"), P("tensor", None)),
        out_specs=(P("tensor", None), P("dp", None, "tensor")),
        check_vma=False,
    )
```

```python
import functools

import jax
import jax.numpy as jnp
from jax import lax
from jax.experimental import pallas as pl
from jax.experimental.pallas import tpu as pltpu
from jax.sharding import PartitionSpec as P

N = 4096
RANK = 64
ITERS = 2
NX, NY, NZ = 4, 4, 8
N_DP = NY * NZ
N_T = 2 * NX
COLS = N // N_T
LANES = 128
PIECES = 3
MESH = pl.DeviceIdType.MESH
HIGH = lax.Precision.HIGHEST
NT = (((1,), (1,)), ((), ()))


def ring_distance(step, size):
    return min(step % size, -step % size)


def distance(o):
    return ring_distance(o[0], NY) + ring_distance(o[1], NZ)


OFFSETS = sorted(
    [(du, dz) for du in range(NY) for dz in range(NZ) if du or dz],
    key=lambda o: -distance(o),
)
FAR_FIRST = (4, 3, 5, 2, 6, 1, 7, 0)
NEAR_FIRST = FAR_FIRST[::-1]
GROUPS = 2 * NZ
ROWS = N // GROUPS


def pieces_of(value):
    out = []
    for _ in range(PIECES):
        piece = value.astype(jnp.bfloat16).astype(jnp.float32)
        out.append(piece)
        value = value - piece
    return out


def split(value):
    return jnp.concatenate([p.astype(jnp.bfloat16) for p in pieces_of(value)], axis=0)


def right_factor(q_t):
    high, mid, low = pieces_of(q_t)
    first = jnp.concatenate([high, mid], axis=0).T
    second = jnp.concatenate([low, jnp.zeros_like(low)], axis=0).T
    return jnp.concatenate([first, second], axis=1).astype(jnp.bfloat16)


def pack(value):
    both = value[:, :LANES] + value[:, LANES:]
    top, bottom = both[:LANES], both[LANES:]
    lower = lax.broadcasted_iota(jnp.int32, (LANES, LANES), 1) < RANK
    kept = jnp.where(lower, top, bottom)
    moved = pltpu.roll(jnp.where(lower, bottom, top), RANK, 1)
    return (kept + moved).reshape(16, 8, LANES)


def unpack_transposed(tiles):
    value = tiles.reshape(LANES, LANES).T
    return jnp.concatenate([value[:RANK], value[RANK:]], axis=1)


def fold(value):
    total = value[0:RANK]
    for i in range(1, PIECES):
        total = total + value[i * RANK : (i + 1) * RANK]
    return total


def to_tiles(value):
    parts = [
        value[:, l * LANES : (l + 1) * LANES].reshape(8, 8, LANES)
        for l in range(value.shape[1] // LANES)
    ]
    return jnp.concatenate(parts, axis=0)


def from_tiles(value):
    parts = [
        value[8 * l : 8 * l + 8].reshape(RANK, LANES)
        for l in range(value.shape[0] // 8)
    ]
    return jnp.concatenate(parts, axis=1)


def eliminate(work, first, last):
    lane = lax.broadcasted_iota(jnp.int32, (RANK, 2 * RANK), 1)
    row = lax.broadcasted_iota(jnp.int32, (RANK, 1), 0)
    lane1 = lax.broadcasted_iota(jnp.int32, (1, 2 * RANK), 1)

    def step(j, carry):
        a = work[...]
        pivot_row = work[pl.ds(j, 1), :]
        pivot = jnp.sum(jnp.where(lane1 == j, pivot_row, 0.0), axis=1, keepdims=True)
        column = jnp.sum(jnp.where(lane == j, a, 0.0), axis=1, keepdims=True)
        column = jnp.where(row > j, column, 0.0)
        work[...] = a - column * (pivot_row / pivot)
        return carry

    lax.fori_loop(first, last, step, 0)


def inverse_factor(work):
    a = work[...]
    lane = lax.broadcasted_iota(jnp.int32, (RANK, 2 * RANK), 1)
    row = lax.broadcasted_iota(jnp.int32, (RANK, 2 * RANK), 0)
    diagonal = jnp.sum(jnp.where(lane == row, a, 0.0), axis=1, keepdims=True)
    return a[:, RANK:] / jnp.sqrt(diagonal)


def kernel(
    g_hbm, e_hbm, q_ref, q_out, g, e, ph,
    qs, pp, sb, xs, xr, acc, yr, pg, qp, qr, qg, work,
    load_sem, sib_send, sib_recv, x_send, x_recv, y_send, y_recv,
    ag_send, ag_recv, xg_send, xg_recv, sg_send, sg_recv,
    qr_send, qr_recv, qa_send, qa_recv,
):
    dp = lax.axis_index("dp")
    t = lax.axis_index("tensor")
    y, z = dp // NZ, dp % NZ
    x, c = t // 2, t % 2
    sibling = (dp, 2 * x + (1 - c))

    def device(y_at, z_at, x_at):
        return (y_at * NZ + z_at, 2 * x_at + c)

    def z_of(dz):
        return (z + dz) % NZ

    def line_place(z_at):
        odd = z_at % 2
        return x * (1 - odd) + y * odd

    def plane_place(z_at):
        odd = z_at % 2
        return y * (1 - odd) + x * odd

    def on_line(place, z_at):
        odd = z_at % 2
        return device(y * (1 - odd) + place * odd, z, place * (1 - odd) + x * odd)

    def on_plane(place, z_at, owner_z):
        odd = owner_z % 2
        return device(place * (1 - odd) + y * odd, z_at, x * (1 - odd) + place * odd)

    dp_peers = [device((y + o[0]) % NY, z_of(o[1]), x) for o in OFFSETS]
    others = [device(y, z_of(o[1]), (x + o[0]) % NX) for o in OFFSETS if o[0]]
    near_x = [o for o in OFFSETS if o[0]]
    by_distance = sorted(
        list(zip(OFFSETS, dp_peers)) + list(zip(near_x, others)),
        key=lambda pair: -distance(pair[0]),
    )
    everyone = [peer for _, peer in by_distance] + [sibling]

    barrier = pltpu.get_barrier_semaphore()
    for peer in everyone:
        pl.semaphore_signal(barrier, inc=1, device_id=peer, device_id_type=MESH)

    def rows_of(core, z_at):
        return pl.ds(pl.multiple_of((core * NZ + z_at) * ROWS, ROWS), ROWS)

    loads = []
    for i, dz in enumerate(FAR_FIRST):
        for core in (1 - c, c):
            rows = rows_of(core, z_of(dz))
            pair = []
            for k, (hbm, vmem) in enumerate(((g_hbm, g), (e_hbm, e))):
                copy = pltpu.make_async_copy(
                    hbm.at[0, rows, :], vmem.at[rows, :], load_sem.at[len(loads), k]
                )
                copy.start()
                pair.append(copy)
            loads.append(pair)

    qs[...] = right_factor(q_ref[...])

    def send(src, dst, send_sem, recv_sem, target):
        pltpu.make_async_remote_copy(
            src_ref=src,
            dst_ref=dst,
            send_sem=send_sem,
            recv_sem=recv_sem,
            device_id=target,
            device_id_type=MESH,
        ).start()

    def wait_bytes(ref, sem):
        pltpu.make_async_copy(ref, ref, sem).wait()

    scale = 1.0 / N_DP
    for it in range(ITERS):

        def p_chunk(core, z_at):
            rows = rows_of(core, z_at)
            factor = qs[...]
            a = jnp.dot(g[rows, :], factor, preferred_element_type=jnp.float32)
            b = jnp.dot(e[rows, :], factor, preferred_element_type=jnp.float32)
            return pack(a + b)

        def pass_along(dz):
            wait_bytes(sb.at[it, dz], sib_recv.at[it, dz])
            xs[it, dz] = xs[it, dz] + sb[it, dz]
            here = line_place(z_of(dz))
            for d in (2, 1, 3):
                place = (here + d) % NX
                send(
                    xs.at[it, dz, pl.ds(4 * place, 4)],
                    xr.at[it, dz, d - 1],
                    x_send.at[it],
                    x_recv.at[it, dz],
                    on_line(place, z_of(dz)),
                )

        def to_sibling(dz):
            send(
                pp.at[it, dz],
                sb.at[it, dz],
                sib_send.at[it],
                sib_recv.at[it, dz],
                sibling,
            )

        if it == 0:
            for i, dz in enumerate(FAR_FIRST):
                for copy in loads[2 * i] + loads[2 * i + 1]:
                    copy.wait()
                pp[it, dz] = p_chunk(1 - c, z_of(dz))
                xs[it, dz] = p_chunk(c, z_of(dz))
            pl.semaphore_wait(barrier, len(everyone))
            for dz in FAR_FIRST:
                to_sibling(dz)
            for dz in FAR_FIRST:
                pass_along(dz)
        else:
            for i, dz in enumerate(FAR_FIRST):
                pp[it, dz] = p_chunk(1 - c, z_of(dz))
                to_sibling(dz)
                xs[it, dz] = p_chunk(c, z_of(dz))
                if i:
                    pass_along(FAR_FIRST[i - 1])
            pass_along(FAR_FIRST[-1])

        slot = 0
        for dz in FAR_FIRST:
            wait_bytes(xr.at[it, dz], x_recv.at[it, dz])
            total = xs[it, dz, pl.ds(4 * line_place(z_of(dz)), 4)]
            for d in (1, 2, 3):
                total = total + xr[it, dz, d - 1]
            acc[it, dz] = total * scale
            for du in (2, 1, 3, 0):
                if not (du or dz):
                    continue
                place = (plane_place(z_of(dz)) + du) % NY
                send(
                    acc.at[it, dz, place],
                    yr.at[it, slot],
                    y_send.at[it],
                    y_recv.at[it],
                    on_plane(place, z_of(dz), z_of(dz)),
                )
                slot += 1

        mine = 4 * line_place(z) + plane_place(z)
        own = acc[it, 0, plane_place(z)]
        wait_bytes(yr.at[it], y_recv.at[it])
        pg[it, c * NZ + z, mine] = own + jnp.sum(yr[it], axis=0)

        for du, dz in OFFSETS:
            tile = pg.at[it, c * NZ + z, mine]
            place = (plane_place(z) + du) % NY
            send(
                tile,
                tile,
                ag_send.at[it],
                ag_recv.at[it, dz],
                on_plane(place, z_of(dz), z),
            )

        for dz in NEAR_FIRST:
            z_at = z_of(-dz)
            here = line_place(z_at)
            tiles = pg.at[it, c * NZ + z_at, pl.ds(4 * here, 4)]
            if dz:
                wait_bytes(tiles, ag_recv.at[it, dz])
            else:
                wait_bytes(yr.at[it, pl.ds(0, 3)], ag_recv.at[it, dz])
            for d in (2, 1, 3):
                send(
                    tiles,
                    tiles,
                    xg_send.at[it],
                    xg_recv.at[it, dz],
                    on_line((here + d) % NX, z_at),
                )

        q_acc = jnp.zeros((RANK, COLS), jnp.float32)
        gram = jnp.zeros((PIECES * RANK, PIECES * RANK), jnp.float32)

        def q_chunk(core, z_at, q_acc, gram):
            rows = rows_of(core, z_at)
            lhs = split(unpack_transposed(pg[it, core * NZ + z_at]))
            a = jnp.dot(lhs, g[rows, :], preferred_element_type=jnp.float32)
            b = jnp.dot(lhs, e[rows, :], preferred_element_type=jnp.float32)
            more = lax.dot_general(lhs, lhs, NT, preferred_element_type=jnp.float32)
            return q_acc + fold(a + b), gram + more

        for dz in NEAR_FIRST:
            z_at = z_of(-dz)
            wait_bytes(xr.at[it, 0], xg_recv.at[it, dz])
            chunk = pg.at[it, c * NZ + z_at]
            send(chunk, chunk, sg_send.at[it], sg_recv.at[it, dz], sibling)
            q_acc, gram = q_chunk(c, z_at, q_acc, gram)
        for dz in NEAR_FIRST:
            z_at = z_of(-dz)
            wait_bytes(pg.at[it, (1 - c) * NZ + z_at], sg_recv.at[it, dz])
            q_acc, gram = q_chunk(1 - c, z_at, q_acc, gram)

        qp[it] = to_tiles(q_acc * scale)
        for k, peer in enumerate(dp_peers):
            send(
                qp.at[it, peer[0]],
                qr.at[it, k],
                qr_send.at[it],
                qr_recv.at[it],
                peer,
            )

        square = jnp.zeros((RANK, RANK), jnp.float32)
        for i in range(PIECES):
            for j in range(PIECES):
                square = square + gram[
                    i * RANK : (i + 1) * RANK, j * RANK : (j + 1) * RANK
                ]
        row = lax.broadcasted_iota(jnp.int32, (RANK, RANK), 0)
        lane = lax.broadcasted_iota(jnp.int32, (RANK, RANK), 1)
        eye = jnp.where(row == lane, 1.0, 0.0)
        work[...] = jnp.concatenate([square, eye], axis=1)
        eliminate(work, 0, RANK // 2)

        wait_bytes(qr.at[it], qr_recv.at[it])
        qg[it, dp] = qp[it, dp] + jnp.sum(qr[it], axis=0)
        for peer in dp_peers:
            send(
                qg.at[it, dp],
                qg.at[it, dp],
                qa_send.at[it],
                qa_recv.at[it],
                peer,
            )
        eliminate(work, RANK // 2, RANK)
        l_inverse = inverse_factor(work)

        if it == ITERS - 1:
            none = jnp.zeros((RANK, RANK), jnp.float32)
            twice = jnp.concatenate(
                [
                    jnp.concatenate([l_inverse, none], axis=1),
                    jnp.concatenate([none, l_inverse], axis=1),
                ],
                axis=0,
            )
            lower = lax.broadcasted_iota(jnp.int32, (LANES, LANES), 1) < RANK
            for i in range(GROUPS):
                hat = lax.dot_general(
                    pg[it, i].reshape(LANES, LANES),
                    twice,
                    NT,
                    precision=HIGH,
                    preferred_element_type=jnp.float32,
                )
                high = hat.astype(jnp.bfloat16).astype(jnp.float32)
                low = hat - high
                top = jnp.where(lower, high, pltpu.roll(low, RANK, 1))
                bottom = jnp.where(lower, pltpu.roll(high, RANK, 1), low)
                both = jnp.concatenate([top, bottom], axis=0).astype(jnp.bfloat16)
                ph[i * ROWS : (i + 1) * ROWS, :] = jnp.concatenate([both, both], axis=1)

        wait_bytes(pp.at[it], sib_send.at[it])
        wait_bytes(xr.at[it], x_send.at[it])
        wait_bytes(yr.at[it], y_send.at[it])
        wait_bytes(yr.at[it], ag_send.at[it])
        wait_bytes(xr.at[it], xg_send.at[it])
        wait_bytes(pp.at[it], sg_send.at[it])
        wait_bytes(qr.at[it], qr_send.at[it])

        wait_bytes(qr.at[it], qa_recv.at[it])
        q_now = jnp.dot(
            l_inverse,
            from_tiles(qg[it]),
            precision=HIGH,
            preferred_element_type=jnp.float32,
        )
        if it < ITERS - 1:
            qs[...] = right_factor(q_now)
        else:
            q_out[...] = q_now

    for it in range(ITERS):
        wait_bytes(qr.at[it], qa_send.at[it])


def finish(g, e, ph, q_ref, q_out, new_out, right):
    step = pl.program_id(0)

    @pl.when(step == 0)
    def _():
        q_now = q_ref[...]
        q_out[...] = q_now
        high = q_now.astype(jnp.bfloat16)
        low = (q_now - high.astype(jnp.float32)).astype(jnp.bfloat16)
        right[...] = jnp.concatenate([high, high, low, low], axis=0)

    rows = pl.ds(pl.multiple_of(step * COLS, COLS), COLS)
    approx = jnp.dot(ph[rows, :], right[...], preferred_element_type=jnp.float32)
    merged = g[rows, :].astype(jnp.float32) + e[rows, :].astype(jnp.float32)
    new_out[0] = (merged - approx).astype(jnp.bfloat16)


def body(gradient, error, q_prev):
    f32, bf16 = jnp.float32, jnp.bfloat16
    dma = pltpu.SemaphoreType.DMA
    vmem = pl.BlockSpec(memory_space=pltpu.VMEM)
    hbm = pl.BlockSpec(memory_space=pltpu.HBM)
    q_t, g, e, p_hat = pl.pallas_call(
        kernel,
        out_shape=(
            jax.ShapeDtypeStruct((RANK, COLS), f32),
            jax.ShapeDtypeStruct((N, COLS), bf16),
            jax.ShapeDtypeStruct((N, COLS), bf16),
            jax.ShapeDtypeStruct((N, 4 * RANK), bf16),
        ),
        in_specs=[hbm, hbm, vmem],
        out_specs=(vmem, vmem, vmem, vmem),
        scratch_shapes=[
            pltpu.VMEM((COLS, 4 * RANK), bf16),
            pltpu.VMEM((ITERS, NZ, 16, 8, LANES), f32),
            pltpu.VMEM((ITERS, NZ, 16, 8, LANES), f32),
            pltpu.VMEM((ITERS, NZ, 16, 8, LANES), f32),
            pltpu.VMEM((ITERS, NZ, 3, 4, 8, LANES), f32),
            pltpu.VMEM((ITERS, NZ, 4, 8, LANES), f32),
            pltpu.VMEM((ITERS, N_DP - 1, 8, LANES), f32),
            pltpu.VMEM((ITERS, GROUPS, 16, 8, LANES), f32),
            pltpu.VMEM((ITERS, N_DP, 8, LANES), f32),
            pltpu.VMEM((ITERS, N_DP - 1, 8, LANES), f32),
            pltpu.VMEM((ITERS, N_DP, 8, LANES), f32),
            pltpu.VMEM((RANK, 2 * RANK), f32),
            dma((GROUPS, 2)),
            dma((ITERS,)),
            dma((ITERS, NZ)),
            dma((ITERS,)),
            dma((ITERS, NZ)),
            dma((ITERS,)),
            dma((ITERS,)),
            dma((ITERS,)),
            dma((ITERS, NZ)),
            dma((ITERS,)),
            dma((ITERS, NZ)),
            dma((ITERS,)),
            dma((ITERS, NZ)),
            dma((ITERS,)),
            dma((ITERS,)),
            dma((ITERS,)),
            dma((ITERS,)),
        ],
        compiler_params=pltpu.CompilerParams(
            collective_id=1, has_side_effects=True, vmem_limit_bytes=41 * 2**20
        ),
    )(gradient, error, q_prev.T)
    q_t, new_error = pl.pallas_call(
        finish,
        grid=(N // COLS,),
        out_shape=(
            jax.ShapeDtypeStruct((RANK, COLS), f32),
            jax.ShapeDtypeStruct((1, N, COLS), bf16),
        ),
        in_specs=[vmem, vmem, vmem, vmem],
        out_specs=(
            pl.BlockSpec((RANK, COLS), lambda i: (0, 0)),
            pl.BlockSpec((1, COLS, COLS), lambda i: (0, i, 0)),
        ),
        scratch_shapes=[pltpu.VMEM((4 * RANK, COLS), bf16)],
        compiler_params=pltpu.CompilerParams(vmem_limit_bytes=24 * 2**20),
    )(g, e, p_hat, q_t)
    return q_t.T, new_error


def solution(mesh):
    return jax.shard_map(
        body,
        mesh=mesh,
        in_specs=(P("dp", None, "tensor"), P("dp", None, "tensor"), P("tensor", None)),
        out_specs=(P("tensor", None), P("dp", None, "tensor")),
        check_vma=False,
    )
```

```python
import functools

import jax
import jax.numpy as jnp
from jax import lax
from jax.experimental import pallas as pl
from jax.experimental.pallas import tpu as pltpu
from jax.sharding import PartitionSpec as P

N = 4096
RANK = 64
ITERS = 2
NX, NY, NZ = 4, 4, 8
N_DP = NY * NZ
N_T = 2 * NX
COLS = N // N_T
LANES = 128
PIECES = 3
EARLY = 48
MESH = pl.DeviceIdType.MESH
HIGH = lax.Precision.HIGHEST
NT = (((1,), (1,)), ((), ()))


def ring_distance(step, size):
    return min(step % size, -step % size)


def distance(o):
    return ring_distance(o[0], NY) + ring_distance(o[1], NZ)


OFFSETS = sorted(
    [(du, dz) for du in range(NY) for dz in range(NZ) if du or dz],
    key=lambda o: -distance(o),
)
SLOTS = (4, 3, 5, 2, 6, 1, 7, 0)
SPANS = ((0, 1), (1, 3), (3, 5), (5, 7), (7, 8))
N_SPANS = len(SPANS)
ROWS = N // (2 * NZ)


def slot_of(dz):
    return SLOTS.index(dz % NZ)


def span_of(dz):
    return N_SPANS - 1 - ring_distance(dz, NZ)


def pieces_of(value):
    out = []
    for _ in range(PIECES):
        piece = value.astype(jnp.bfloat16).astype(jnp.float32)
        out.append(piece)
        value = value - piece
    return out


def split(value):
    return jnp.concatenate([p.astype(jnp.bfloat16) for p in pieces_of(value)], axis=0)


def right_factor(q_t):
    high, mid, low = pieces_of(q_t)
    first = jnp.concatenate([high, mid], axis=0).T
    second = jnp.concatenate([low, jnp.zeros_like(low)], axis=0).T
    return jnp.concatenate([first, second], axis=1).astype(jnp.bfloat16)


def pack(value):
    both = value[:, :LANES] + value[:, LANES:]
    top, bottom = both[:LANES], both[LANES:]
    lower = lax.broadcasted_iota(jnp.int32, (LANES, LANES), 1) < RANK
    kept = jnp.where(lower, top, bottom)
    moved = pltpu.roll(jnp.where(lower, bottom, top), RANK, 1)
    return (kept + moved).reshape(16, 8, LANES)


def unpack_transposed(tiles):
    value = tiles.reshape(LANES, LANES).T
    return jnp.concatenate([value[:RANK], value[RANK:]], axis=1)


def fold(value):
    total = value[0:RANK]
    for i in range(1, PIECES):
        total = total + value[i * RANK : (i + 1) * RANK]
    return total


def to_tiles(value):
    parts = [
        value[:, l * LANES : (l + 1) * LANES].reshape(8, 8, LANES)
        for l in range(value.shape[1] // LANES)
    ]
    return jnp.concatenate(parts, axis=0)


def from_tiles(value):
    parts = [
        value[8 * l : 8 * l + 8].reshape(RANK, LANES)
        for l in range(value.shape[0] // 8)
    ]
    return jnp.concatenate(parts, axis=1)


def eliminate(work, first, last):
    lane = lax.broadcasted_iota(jnp.int32, (RANK, 2 * RANK), 1)
    row = lax.broadcasted_iota(jnp.int32, (RANK, 1), 0)
    lane1 = lax.broadcasted_iota(jnp.int32, (1, 2 * RANK), 1)

    def step(j, carry):
        a = work[...]
        pivot_row = work[pl.ds(j, 1), :]
        pivot = jnp.sum(jnp.where(lane1 == j, pivot_row, 0.0), axis=1, keepdims=True)
        column = jnp.sum(jnp.where(lane == j, a, 0.0), axis=1, keepdims=True)
        column = jnp.where(row > j, column, 0.0)
        work[...] = a - column * (pivot_row / pivot)
        return carry

    lax.fori_loop(first, last, step, 0)


def inverse_factor(work):
    a = work[...]
    lane = lax.broadcasted_iota(jnp.int32, (RANK, 2 * RANK), 1)
    row = lax.broadcasted_iota(jnp.int32, (RANK, 2 * RANK), 0)
    diagonal = jnp.sum(jnp.where(lane == row, a, 0.0), axis=1, keepdims=True)
    return a[:, RANK:] / jnp.sqrt(diagonal)


def kernel(
    g_hbm, e_hbm, q_ref, q_out, g, e, ph,
    qs, pp, sb, xs, xr, acc, yr, pg, qp, qr, qg, work,
    load_sem, sib_send, sib_recv, x_send, x_recv, y_send, y_recv,
    ag_send, ag_recv, xg_send, xg_recv, sg_send, sg_recv,
    qr_send, qr_recv, qa_send, qa_recv,
):
    dp = lax.axis_index("dp")
    t = lax.axis_index("tensor")
    y, z = lax.div(dp, NZ), lax.rem(dp, NZ)
    x, c = lax.div(t, 2), lax.rem(t, 2)
    sibling = (dp, t + 1 - 2 * c)

    def around(place, step, size):
        return lax.rem(place + step % size, size)

    xs_at = [around(x, d, NX) for d in range(NX)]
    ys_at = [around(y, d, NY) for d in range(NY)]
    zs_at = [around(z, d, NZ) for d in range(NZ)]

    odd = lax.rem(z, 2)
    odds = (odd, 1 - odd)

    def device(y_at, z_at, x_at):
        return (y_at * NZ + z_at, 2 * x_at + c)

    def either(k, even_case, odd_case):
        return even_case * (1 - odds[k]) + odd_case * odds[k]

    line_place = [[either(k, xs_at[d], ys_at[d]) for d in range(NX)] for k in (0, 1)]
    plane_place = [line_place[1], line_place[0]]
    line_device = [
        [device(either(k, y, ys_at[d]), z, either(k, xs_at[d], x)) for d in range(NX)]
        for k in (0, 1)
    ]

    def plane_device(k, du, dz):
        return device(either(k, ys_at[du], y), zs_at[dz], either(k, x, xs_at[du]))

    own_plane = {o: plane_device(0, *o) for o in OFFSETS}
    other_plane = {o: plane_device(1, *o) for o in OFFSETS}
    dp_peers = [device(ys_at[o[0]], zs_at[o[1]], x) for o in OFFSETS]

    everyone = []
    for o in OFFSETS:
        everyone.append(own_plane[o])
        if o[0]:
            everyone.append(other_plane[o])
    everyone.append(sibling)

    barrier = pltpu.get_barrier_semaphore()
    for peer in everyone:
        pl.semaphore_signal(barrier, inc=1, device_id=peer, device_id_type=MESH)

    def rows_of(core, slot):
        start = (core * NZ + zs_at[SLOTS[slot]]) * ROWS
        return pl.ds(pl.multiple_of(start, ROWS), ROWS)

    loads = []
    for slot in range(NZ):
        copies = []
        for i, core in enumerate((1 - c, c)):
            rows = rows_of(core, slot)
            for k, (hbm, vmem) in enumerate(((g_hbm, g), (e_hbm, e))):
                copy = pltpu.make_async_copy(
                    hbm.at[0, rows, :], vmem.at[rows, :], load_sem.at[slot, 2 * i + k]
                )
                copy.start()
                copies.append(copy)
        loads.append(copies)

    qs[...] = right_factor(q_ref[...])

    def send(src, dst, send_sem, recv_sem, target):
        pltpu.make_async_remote_copy(
            src_ref=src,
            dst_ref=dst,
            send_sem=send_sem,
            recv_sem=recv_sem,
            device_id=target,
            device_id_type=MESH,
        ).start()

    def wait_bytes(ref, sem):
        pltpu.make_async_copy(ref, ref, sem).wait()

    scale = 1.0 / N_DP
    for it in range(ITERS):

        def p_rows(core, slot):
            rows = rows_of(core, slot)
            factor = qs[...]
            a = jnp.dot(g[rows, :], factor, preferred_element_type=jnp.float32)
            b = jnp.dot(e[rows, :], factor, preferred_element_type=jnp.float32)
            return pack(a + b)

        def for_sibling(span):
            for slot in range(*SPANS[span]):
                pp[it, slot] = p_rows(1 - c, slot)

        def for_own(span):
            for slot in range(*SPANS[span]):
                xs[it, slot] = p_rows(c, slot)

        def slots(span):
            return pl.ds(SPANS[span][0], SPANS[span][1] - SPANS[span][0])

        def to_sibling(span):
            send(
                pp.at[it, slots(span)],
                sb.at[it, slots(span)],
                sib_send.at[it],
                sib_recv.at[it, span],
                sibling,
            )

        def to_line(span):
            wait_bytes(sb.at[it, slots(span)], sib_recv.at[it, span])
            for slot in range(*SPANS[span]):
                xs[it, slot] = xs[it, slot] + sb[it, slot]
            k = span % 2
            for d in (2, 1, 3):
                send(
                    xs.at[it, slots(span), pl.ds(4 * line_place[k][d], 4)],
                    xr.at[it, d - 1, slots(span)],
                    x_send.at[it],
                    x_recv.at[it, span],
                    line_device[k][d],
                )

        def to_plane(span):
            wait_bytes(xr.at[it, :, slots(span)], x_recv.at[it, span])
            k = span % 2
            for slot in range(*SPANS[span]):
                total = xs[it, slot, pl.ds(4 * line_place[k][0], 4)]
                for d in (1, 2, 3):
                    total = total + xr[it, d - 1, slot]
                acc[it, slot] = total * scale
            for du in (2, 1, 3, 0):
                for slot in range(*SPANS[span]):
                    o = (du, SLOTS[slot])
                    if o == (0, 0):
                        continue
                    send(
                        acc.at[it, slot, plane_place[k][du]],
                        yr.at[it, OFFSETS.index(o)],
                        y_send.at[it],
                        y_recv.at[it],
                        (own_plane, other_plane)[k][o],
                    )

        if it == 0:
            for span in range(N_SPANS):
                for slot in range(*SPANS[span]):
                    for copy in loads[slot]:
                        copy.wait()
                for_sibling(span)
                for_own(span)
            pl.semaphore_wait(barrier, len(everyone))
            for span in range(N_SPANS):
                to_sibling(span)
            to_line(0)
            to_line(1)
            to_line(2)
            to_plane(0)
            to_line(3)
            to_plane(1)
            to_line(4)
        else:
            for span in range(N_SPANS):
                for_sibling(span)
                to_sibling(span)
                for_own(span)
                if span:
                    to_line(span - 1)
                if span == 3:
                    to_plane(0)
            to_plane(1)
            to_line(4)
        to_plane(2)
        to_plane(3)
        to_plane(4)

        near = slot_of(0)
        mine = 4 * line_place[0][0] + plane_place[0][0]
        own = acc[it, near, plane_place[0][0]]
        wait_bytes(yr.at[it], y_recv.at[it])
        pg[it, c, near, mine] = own + jnp.sum(yr[it], axis=0)

        for o in OFFSETS:
            send(
                pg.at[it, c, near, mine],
                pg.at[it, c, slot_of(-o[1]), mine],
                ag_send.at[it],
                ag_recv.at[it, span_of(o[1])],
                own_plane[o],
            )

        for span in range(N_SPANS - 1, -1, -1):
            k = span % 2
            tiles = pg.at[it, c, slots(span), pl.ds(4 * line_place[k][0], 4)]
            if span == N_SPANS - 1:
                wait_bytes(yr.at[it, pl.ds(0, 3)], ag_recv.at[it, span])
            else:
                wait_bytes(tiles, ag_recv.at[it, span])
            for d in (2, 1, 3):
                send(
                    tiles, tiles, xg_send.at[it], xg_recv.at[it, span], line_device[k][d]
                )

        q_acc = jnp.zeros((RANK, COLS), jnp.float32)
        gram = jnp.zeros((PIECES * RANK, PIECES * RANK), jnp.float32)

        def q_rows(core, span, q_acc, gram):
            for slot in range(*SPANS[span]):
                rows = rows_of(core, slot)
                lhs = split(unpack_transposed(pg[it, core, slot]))
                a = jnp.dot(lhs, g[rows, :], preferred_element_type=jnp.float32)
                b = jnp.dot(lhs, e[rows, :], preferred_element_type=jnp.float32)
                more = lax.dot_general(
                    lhs, lhs, NT, preferred_element_type=jnp.float32
                )
                q_acc, gram = q_acc + fold(a + b), gram + more
            return q_acc, gram

        for span in range(N_SPANS - 1, -1, -1):
            wait_bytes(xr.at[it, :, slots(span)], xg_recv.at[it, span])
            chunk = pg.at[it, c, slots(span)]
            send(chunk, chunk, sg_send.at[it], sg_recv.at[it, span], sibling)
            q_acc, gram = q_rows(c, span, q_acc, gram)
        for span in range(N_SPANS - 1, -1, -1):
            wait_bytes(pg.at[it, 1 - c, slots(span)], sg_recv.at[it, span])
            q_acc, gram = q_rows(1 - c, span, q_acc, gram)

        qp[it] = to_tiles(q_acc * scale)
        for k, peer in enumerate(dp_peers):
            send(
                qp.at[it, peer[0]],
                qr.at[it, k],
                qr_send.at[it],
                qr_recv.at[it],
                peer,
            )

        square = jnp.zeros((RANK, RANK), jnp.float32)
        for i in range(PIECES):
            for j in range(PIECES):
                square = square + gram[
                    i * RANK : (i + 1) * RANK, j * RANK : (j + 1) * RANK
                ]
        row = lax.broadcasted_iota(jnp.int32, (RANK, RANK), 0)
        lane = lax.broadcasted_iota(jnp.int32, (RANK, RANK), 1)
        eye = jnp.where(row == lane, 1.0, 0.0)
        work[...] = jnp.concatenate([square, eye], axis=1)
        eliminate(work, 0, EARLY)

        wait_bytes(qr.at[it], qr_recv.at[it])
        qg[it, dp] = qp[it, dp] + jnp.sum(qr[it], axis=0)
        for peer in dp_peers:
            send(
                qg.at[it, dp],
                qg.at[it, dp],
                qa_send.at[it],
                qa_recv.at[it],
                peer,
            )
        eliminate(work, EARLY, RANK)
        l_inverse = inverse_factor(work)

        if it == ITERS - 1:
            none = jnp.zeros((RANK, RANK), jnp.float32)
            twice = jnp.concatenate(
                [
                    jnp.concatenate([l_inverse, none], axis=1),
                    jnp.concatenate([none, l_inverse], axis=1),
                ],
                axis=0,
            )
            lower = lax.broadcasted_iota(jnp.int32, (LANES, LANES), 1) < RANK
            for i in range(2 * NZ):
                hat = lax.dot_general(
                    pg[it, i // NZ, i % NZ].reshape(LANES, LANES),
                    twice,
                    NT,
                    precision=HIGH,
                    preferred_element_type=jnp.float32,
                )
                high = hat.astype(jnp.bfloat16).astype(jnp.float32)
                low = hat - high
                top = jnp.where(lower, high, pltpu.roll(low, RANK, 1))
                bottom = jnp.where(lower, pltpu.roll(high, RANK, 1), low)
                both = jnp.concatenate([top, bottom], axis=0).astype(jnp.bfloat16)
                ph[rows_of(i // NZ, i % NZ), :] = jnp.concatenate([both, both], axis=1)

        wait_bytes(pp.at[it], sib_send.at[it])
        wait_bytes(xr.at[it], x_send.at[it])
        wait_bytes(yr.at[it], y_send.at[it])
        wait_bytes(yr.at[it], ag_send.at[it])
        wait_bytes(xr.at[it], xg_send.at[it])
        wait_bytes(pp.at[it], sg_send.at[it])
        wait_bytes(qr.at[it], qr_send.at[it])

        wait_bytes(qr.at[it], qa_recv.at[it])
        q_now = jnp.dot(
            l_inverse,
            from_tiles(qg[it]),
            precision=HIGH,
            preferred_element_type=jnp.float32,
        )
        if it < ITERS - 1:
            qs[...] = right_factor(q_now)
        else:
            q_out[...] = q_now

    for it in range(ITERS):
        wait_bytes(qr.at[it], qa_send.at[it])


def finish(g, e, ph, q_ref, q_out, new_out, buffer, sem):
    copies = [pltpu.make_async_copy(q_ref, q_out, sem.at[2 * NZ])]
    copies[0].start()
    q_now = q_ref[...]
    high = q_now.astype(jnp.bfloat16)
    low = (q_now - high.astype(jnp.float32)).astype(jnp.bfloat16)
    right = jnp.concatenate([high, high, low, low], axis=0)
    for i in range(2 * NZ):
        rows = slice(i * ROWS, (i + 1) * ROWS)
        approx = jnp.dot(ph[rows, :], right, preferred_element_type=jnp.float32)
        merged = g[rows, :].astype(jnp.float32) + e[rows, :].astype(jnp.float32)
        buffer[rows, :] = (merged - approx).astype(jnp.bfloat16)
        copy = pltpu.make_async_copy(
            buffer.at[rows, :], new_out.at[0, rows, :], sem.at[i]
        )
        copy.start()
        copies.append(copy)
    for copy in copies:
        copy.wait()


def body(gradient, error, q_prev):
    f32, bf16 = jnp.float32, jnp.bfloat16
    dma = pltpu.SemaphoreType.DMA
    vmem = pl.BlockSpec(memory_space=pltpu.VMEM)
    hbm = pl.BlockSpec(memory_space=pltpu.HBM)
    q_t, g, e, p_hat = pl.pallas_call(
        kernel,
        out_shape=(
            jax.ShapeDtypeStruct((RANK, COLS), f32),
            jax.ShapeDtypeStruct((N, COLS), bf16),
            jax.ShapeDtypeStruct((N, COLS), bf16),
            jax.ShapeDtypeStruct((N, 4 * RANK), bf16),
        ),
        in_specs=[hbm, hbm, vmem],
        out_specs=(vmem, vmem, vmem, vmem),
        scratch_shapes=[
            pltpu.VMEM((COLS, 4 * RANK), bf16),
            pltpu.VMEM((ITERS, NZ, 16, 8, LANES), f32),
            pltpu.VMEM((ITERS, NZ, 16, 8, LANES), f32),
            pltpu.VMEM((ITERS, NZ, 16, 8, LANES), f32),
            pltpu.VMEM((ITERS, 3, NZ, 4, 8, LANES), f32),
            pltpu.VMEM((ITERS, NZ, 4, 8, LANES), f32),
            pltpu.VMEM((ITERS, N_DP - 1, 8, LANES), f32),
            pltpu.VMEM((ITERS, 2, NZ, 16, 8, LANES), f32),
            pltpu.VMEM((ITERS, N_DP, 8, LANES), f32),
            pltpu.VMEM((ITERS, N_DP - 1, 8, LANES), f32),
            pltpu.VMEM((ITERS, N_DP, 8, LANES), f32),
            pltpu.VMEM((RANK, 2 * RANK), f32),
            dma((NZ, 4)),
            dma((ITERS,)),
            dma((ITERS, N_SPANS)),
            dma((ITERS,)),
            dma((ITERS, N_SPANS)),
            dma((ITERS,)),
            dma((ITERS,)),
            dma((ITERS,)),
            dma((ITERS, N_SPANS)),
            dma((ITERS,)),
            dma((ITERS, N_SPANS)),
            dma((ITERS,)),
            dma((ITERS, N_SPANS)),
            dma((ITERS,)),
            dma((ITERS,)),
            dma((ITERS,)),
            dma((ITERS,)),
        ],
        compiler_params=pltpu.CompilerParams(
            collective_id=1, has_side_effects=True, vmem_limit_bytes=41 * 2**20
        ),
    )(gradient, error, q_prev.T)
    q_t, new_error = pl.pallas_call(
        finish,
        out_shape=(
            jax.ShapeDtypeStruct((RANK, COLS), f32),
            jax.ShapeDtypeStruct((1, N, COLS), bf16),
        ),
        in_specs=[vmem, vmem, vmem, vmem],
        out_specs=(
            pl.BlockSpec(memory_space=pl.ANY),
            pl.BlockSpec(memory_space=pl.ANY),
        ),
        scratch_shapes=[pltpu.VMEM((N, COLS), bf16), dma((2 * NZ + 1,))],
        compiler_params=pltpu.CompilerParams(vmem_limit_bytes=40 * 2**20),
    )(g, e, p_hat, q_t)
    return q_t.T, new_error


def solution(mesh):
    return jax.shard_map(
        body,
        mesh=mesh,
        in_specs=(P("dp", None, "tensor"), P("dp", None, "tensor"), P("tensor", None)),
        out_specs=(P("tensor", None), P("dp", None, "tensor")),
        check_vma=False,
    )
```

```python
import functools

import jax
import jax.numpy as jnp
from jax import lax
from jax.experimental import pallas as pl
from jax.experimental.pallas import tpu as pltpu
from jax.sharding import PartitionSpec as P

N = 4096
RANK = 64
ITERS = 2
NX, NY, NZ = 4, 4, 8
N_DP = NY * NZ
N_T = 2 * NX
COLS = N // N_T
LANES = 128
PIECES = 3
EARLY = 48
DIRECT = (0, 1)
SKIP = (0, 1)
SKIPPED = 3
LAG = 5
MESH = pl.DeviceIdType.MESH
HIGH = lax.Precision.HIGHEST
NT = (((1,), (1,)), ((), ()))


def ring_distance(step, size):
    return min(step % size, -step % size)


def distance(o):
    return ring_distance(o[0], NY) + ring_distance(o[1], NZ)


OFFSETS = sorted(
    [(du, dz) for du in range(NY) for dz in range(NZ) if du or dz],
    key=lambda o: -distance(o),
)
SLOTS = (4, 3, 5, 2, 6, 1, 7, 0)
SPANS = ((0, 1), (1, 3), (3, 5), (5, 7), (7, 8))
N_SPANS = len(SPANS)
ROWS = N // (2 * NZ)


def slot_of(dz):
    return SLOTS.index(dz % NZ)


def span_of(dz):
    return N_SPANS - 1 - ring_distance(dz, NZ)


def pieces_of(value):
    out = []
    for _ in range(PIECES):
        piece = value.astype(jnp.bfloat16).astype(jnp.float32)
        out.append(piece)
        value = value - piece
    return out


def split(value):
    return jnp.concatenate([p.astype(jnp.bfloat16) for p in pieces_of(value)], axis=0)


def right_factor(q_t):
    high, mid, low = pieces_of(q_t)
    first = jnp.concatenate([high, mid], axis=0).T
    second = jnp.concatenate([low, jnp.zeros_like(low)], axis=0).T
    return jnp.concatenate([first, second], axis=1).astype(jnp.bfloat16)


def pack(value):
    both = value[:, :LANES] + value[:, LANES:]
    top, bottom = both[:LANES], both[LANES:]
    lower = lax.broadcasted_iota(jnp.int32, (LANES, LANES), 1) < RANK
    kept = jnp.where(lower, top, bottom)
    moved = pltpu.roll(jnp.where(lower, bottom, top), RANK, 1)
    return (kept + moved).reshape(16, 8, LANES)


def unpack_transposed(tiles):
    value = tiles.reshape(LANES, LANES).T
    return jnp.concatenate([value[:RANK], value[RANK:]], axis=1)


def fold(value):
    total = value[0:RANK]
    for i in range(1, PIECES):
        total = total + value[i * RANK : (i + 1) * RANK]
    return total


def to_tiles(value):
    parts = [
        value[:, l * LANES : (l + 1) * LANES].reshape(8, 8, LANES)
        for l in range(value.shape[1] // LANES)
    ]
    return jnp.concatenate(parts, axis=0)


def from_tiles(value):
    parts = [
        value[8 * l : 8 * l + 8].reshape(RANK, LANES)
        for l in range(value.shape[0] // 8)
    ]
    return jnp.concatenate(parts, axis=1)


def eliminate(work, first, last):
    lane = lax.broadcasted_iota(jnp.int32, (RANK, 2 * RANK), 1)
    row = lax.broadcasted_iota(jnp.int32, (RANK, 1), 0)
    lane1 = lax.broadcasted_iota(jnp.int32, (1, 2 * RANK), 1)

    def step(j, carry):
        a = work[...]
        pivot_row = work[pl.ds(j, 1), :]
        pivot = jnp.sum(jnp.where(lane1 == j, pivot_row, 0.0), axis=1, keepdims=True)
        column = jnp.sum(jnp.where(lane == j, a, 0.0), axis=1, keepdims=True)
        column = jnp.where(row > j, column, 0.0)
        work[...] = a - column * (pivot_row / pivot)
        return carry

    lax.fori_loop(first, last, step, 0)


def inverse_factor(work):
    a = work[...]
    lane = lax.broadcasted_iota(jnp.int32, (RANK, 2 * RANK), 1)
    row = lax.broadcasted_iota(jnp.int32, (RANK, 2 * RANK), 0)
    diagonal = jnp.sum(jnp.where(lane == row, a, 0.0), axis=1, keepdims=True)
    return a[:, RANK:] / jnp.sqrt(diagonal)


def kernel(
    g_hbm, e_hbm, q_ref, q_out, g, e, ph,
    qs, pp, sb, xs, xr, x2r, acc, yr, pg, qp, qr, qg, work,
    load_sem, sib_send, sib_recv, x_send, x_recv, x2_send, x2_recv, y_send, y_recv,
    ag_send, ag_recv, xg_send, xg_recv, sg_send, sg_recv,
    qr_send, qr_recv, qa_send, qa_recv,
):
    dp = lax.axis_index("dp")
    t = lax.axis_index("tensor")
    y, z = lax.div(dp, NZ), lax.rem(dp, NZ)
    x, c = lax.div(t, 2), lax.rem(t, 2)
    sibling = (dp, t + 1 - 2 * c)

    def around(place, step, size):
        return lax.rem(place + step % size, size)

    xs_at = [around(x, d, NX) for d in range(NX)]
    ys_at = [around(y, d, NY) for d in range(NY)]
    zs_at = [around(z, d, NZ) for d in range(NZ)]

    odd = lax.rem(z, 2)
    odds = (odd, 1 - odd)

    def device(y_at, z_at, x_at):
        return (y_at * NZ + z_at, 2 * x_at + c)

    def either(k, even_case, odd_case):
        return even_case * (1 - odds[k]) + odd_case * odds[k]

    line_place = [[either(k, xs_at[d], ys_at[d]) for d in range(NX)] for k in (0, 1)]
    plane_place = [line_place[1], line_place[0]]
    line_device = [
        [device(either(k, y, ys_at[d]), z, either(k, xs_at[d], x)) for d in range(NX)]
        for k in (0, 1)
    ]

    line_other_core = [
        [(line_device[k][d][0], line_device[k][d][1] + 1 - 2 * c) for d in range(NX)]
        for k in (0, 1)
    ]

    def plane_device(k, du, dz):
        return device(either(k, ys_at[du], y), zs_at[dz], either(k, x, xs_at[du]))

    own_plane = {o: plane_device(0, *o) for o in OFFSETS}
    other_plane = {o: plane_device(1, *o) for o in OFFSETS}
    dp_peers = [device(ys_at[o[0]], zs_at[o[1]], x) for o in OFFSETS]

    everyone = []
    for o in OFFSETS:
        everyone.append(own_plane[o])
        if o[0]:
            everyone.append(other_plane[o])
    everyone.append(sibling)
    everyone += [line_other_core[k][d] for k in (0, 1) for d in (1, 2, 3)]

    barrier = pltpu.get_barrier_semaphore()
    for peer in everyone:
        pl.semaphore_signal(barrier, inc=1, device_id=peer, device_id_type=MESH)

    def rows_of(core, slot):
        start = (core * NZ + zs_at[SLOTS[slot]]) * ROWS
        return pl.ds(pl.multiple_of(start, ROWS), ROWS)

    loads = []
    for slot in range(NZ):
        copies = []
        for i, core in enumerate((1 - c, c)):
            rows = rows_of(core, slot)
            for k, (hbm, vmem) in enumerate(((g_hbm, g), (e_hbm, e))):
                copy = pltpu.make_async_copy(
                    hbm.at[0, rows, :], vmem.at[rows, :], load_sem.at[slot, 2 * i + k]
                )
                copy.start()
                copies.append(copy)
        loads.append(copies)

    qs[...] = right_factor(q_ref[...])

    def send(src, dst, send_sem, recv_sem, target):
        pltpu.make_async_remote_copy(
            src_ref=src,
            dst_ref=dst,
            send_sem=send_sem,
            recv_sem=recv_sem,
            device_id=target,
            device_id_type=MESH,
        ).start()

    def wait_bytes(ref, sem):
        pltpu.make_async_copy(ref, ref, sem).wait()

    scale = 1.0 / N_DP
    for it in range(ITERS):

        def p_rows(core, slot):
            rows = rows_of(core, slot)
            factor = qs[...]
            a = jnp.dot(g[rows, :], factor, preferred_element_type=jnp.float32)
            b = jnp.dot(e[rows, :], factor, preferred_element_type=jnp.float32)
            return pack(a + b)

        def for_sibling(span):
            for slot in range(*SPANS[span]):
                pp[it, slot] = p_rows(1 - c, slot)

        def for_own(span):
            for slot in range(*SPANS[span]):
                xs[it, slot] = p_rows(c, slot)

        def slots(span):
            return pl.ds(SPANS[span][0], SPANS[span][1] - SPANS[span][0])

        def to_sibling(span):
            if span in SKIP:
                return
            send(
                pp.at[it, slots(span)],
                sb.at[it, slots(span)],
                sib_send.at[it],
                sib_recv.at[it, span],
                sibling,
            )

        def to_line(span):
            k = span % 2
            if span in SKIP:
                for d in (2, 1, 3, 0):
                    send(
                        pp.at[it, slots(span), pl.ds(4 * line_place[k][d], 4)],
                        x2r.at[it, d, slots(span)],
                        x2_send.at[it],
                        x2_recv.at[it, span],
                        line_other_core[k][d],
                    )
            else:
                wait_bytes(sb.at[it, slots(span)], sib_recv.at[it, span])
                for slot in range(*SPANS[span]):
                    xs[it, slot] = xs[it, slot] + sb[it, slot]
            for d in (2, 1, 3):
                send(
                    xs.at[it, slots(span), pl.ds(4 * line_place[k][d], 4)],
                    xr.at[it, d - 1, slots(span)],
                    x_send.at[it],
                    x_recv.at[it, span],
                    line_device[k][d],
                )

        def to_plane(span):
            wait_bytes(xr.at[it, :, slots(span)], x_recv.at[it, span])
            if span in SKIP:
                wait_bytes(x2r.at[it, :, slots(span)], x2_recv.at[it, span])
            k = span % 2
            for slot in range(*SPANS[span]):
                total = xs[it, slot, pl.ds(4 * line_place[k][0], 4)]
                for d in (1, 2, 3):
                    total = total + xr[it, d - 1, slot]
                if span in SKIP:
                    for d in range(NX):
                        total = total + x2r[it, d, slot]
                acc[it, slot] = total * scale
            for du in (2, 1, 3, 0):
                for slot in range(*SPANS[span]):
                    o = (du, SLOTS[slot])
                    if o == (0, 0):
                        continue
                    send(
                        acc.at[it, slot, plane_place[k][du]],
                        yr.at[it, OFFSETS.index(o)],
                        y_send.at[it],
                        y_recv.at[it],
                        (own_plane, other_plane)[k][o],
                    )

        if it == 0:
            for span in range(N_SPANS):
                for slot in range(*SPANS[span]):
                    for copy in loads[slot]:
                        copy.wait()
                for_sibling(span)
                for_own(span)
            pl.semaphore_wait(barrier, len(everyone))
            for span in range(N_SPANS):
                to_sibling(span)
            for span in range(N_SPANS):
                to_line(span)
        else:
            for span in SKIP:
                for_sibling(span)
                for_own(span)
                to_line(span)
            rest = [span for span in range(N_SPANS) if span not in SKIP]
            for span in rest:
                for_sibling(span)
                to_sibling(span)
            for i, span in enumerate(rest):
                for_own(span)
                if i:
                    to_line(rest[i - 1])
            to_line(rest[-1])
        for span in range(N_SPANS):
            to_plane(span)

        near = slot_of(0)
        mine = 4 * line_place[0][0] + plane_place[0][0]
        own = acc[it, near, plane_place[0][0]]
        wait_bytes(yr.at[it], y_recv.at[it])
        pg[it, c, near, mine] = own + jnp.sum(yr[it], axis=0)

        for o in OFFSETS:
            send(
                pg.at[it, c, near, mine],
                pg.at[it, c, slot_of(-o[1]), mine],
                ag_send.at[it],
                ag_recv.at[it, span_of(o[1])],
                own_plane[o],
            )

        for span in range(N_SPANS - 1, -1, -1):
            k = span % 2
            tiles = pg.at[it, c, slots(span), pl.ds(4 * line_place[k][0], 4)]
            if span == N_SPANS - 1:
                wait_bytes(yr.at[it, pl.ds(0, 3)], ag_recv.at[it, span])
            else:
                wait_bytes(tiles, ag_recv.at[it, span])
            for d in (2, 1, 3):
                send(
                    tiles, tiles, xg_send.at[it], xg_recv.at[it, span], line_device[k][d]
                )
            if span in DIRECT:
                for target in [line_other_core[k][d] for d in (2, 1, 3)] + [sibling]:
                    send(tiles, tiles, sg_send.at[it], sg_recv.at[it, span], target)

        q_acc = jnp.zeros((RANK, COLS), jnp.float32)
        gram = jnp.zeros((PIECES * RANK, PIECES * RANK), jnp.float32)

        def q_rows(core, span, q_acc, gram):
            for slot in range(*SPANS[span]):
                rows = rows_of(core, slot)
                lhs = split(unpack_transposed(pg[it, core, slot]))
                a = jnp.dot(lhs, g[rows, :], preferred_element_type=jnp.float32)
                b = jnp.dot(lhs, e[rows, :], preferred_element_type=jnp.float32)
                more = lax.dot_general(
                    lhs, lhs, NT, preferred_element_type=jnp.float32
                )
                q_acc, gram = q_acc + fold(a + b), gram + more
            return q_acc, gram

        def sibling_q(span, q_acc, gram):
            wait_bytes(pg.at[it, 1 - c, slots(span)], sg_recv.at[it, span])
            return q_rows(1 - c, span, q_acc, gram)

        for span in range(N_SPANS - 1, -1, -1):
            wait_bytes(xr.at[it, :, slots(span)], xg_recv.at[it, span])
            if span not in DIRECT:
                chunk = pg.at[it, c, slots(span)]
                send(chunk, chunk, sg_send.at[it], sg_recv.at[it, span], sibling)
            q_acc, gram = q_rows(c, span, q_acc, gram)
            if span + LAG < N_SPANS:
                q_acc, gram = sibling_q(span + LAG, q_acc, gram)
        for span in range(LAG - 1, -1, -1):
            q_acc, gram = sibling_q(span, q_acc, gram)

        qp[it] = to_tiles(q_acc * scale)
        for k, peer in enumerate(dp_peers):
            send(
                qp.at[it, peer[0]],
                qr.at[it, k],
                qr_send.at[it],
                qr_recv.at[it],
                peer,
            )

        square = jnp.zeros((RANK, RANK), jnp.float32)
        for i in range(PIECES):
            for j in range(PIECES):
                square = square + gram[
                    i * RANK : (i + 1) * RANK, j * RANK : (j + 1) * RANK
                ]
        row = lax.broadcasted_iota(jnp.int32, (RANK, RANK), 0)
        lane = lax.broadcasted_iota(jnp.int32, (RANK, RANK), 1)
        eye = jnp.where(row == lane, 1.0, 0.0)
        work[...] = jnp.concatenate([square, eye], axis=1)
        eliminate(work, 0, EARLY)

        wait_bytes(qr.at[it], qr_recv.at[it])
        qg[it, dp] = qp[it, dp] + jnp.sum(qr[it], axis=0)
        for peer in dp_peers:
            send(
                qg.at[it, dp],
                qg.at[it, dp],
                qa_send.at[it],
                qa_recv.at[it],
                peer,
            )
        eliminate(work, EARLY, RANK)
        l_inverse = inverse_factor(work)

        if it == ITERS - 1:
            none = jnp.zeros((RANK, RANK), jnp.float32)
            twice = jnp.concatenate(
                [
                    jnp.concatenate([l_inverse, none], axis=1),
                    jnp.concatenate([none, l_inverse], axis=1),
                ],
                axis=0,
            )
            lower = lax.broadcasted_iota(jnp.int32, (LANES, LANES), 1) < RANK
            for i in range(2 * NZ):
                hat = lax.dot_general(
                    pg[it, i // NZ, i % NZ].reshape(LANES, LANES),
                    twice,
                    NT,
                    precision=HIGH,
                    preferred_element_type=jnp.float32,
                )
                high = hat.astype(jnp.bfloat16).astype(jnp.float32)
                low = hat - high
                top = jnp.where(lower, high, pltpu.roll(low, RANK, 1))
                bottom = jnp.where(lower, pltpu.roll(high, RANK, 1), low)
                both = jnp.concatenate([top, bottom], axis=0).astype(jnp.bfloat16)
                ph[rows_of(i // NZ, i % NZ), :] = jnp.concatenate([both, both], axis=1)

        wait_bytes(pp.at[it, pl.ds(SKIPPED, NZ - SKIPPED)], sib_send.at[it])
        wait_bytes(x2r.at[it], x2_send.at[it])
        wait_bytes(xr.at[it], x_send.at[it])
        wait_bytes(yr.at[it], y_send.at[it])
        wait_bytes(yr.at[it], ag_send.at[it])
        wait_bytes(xr.at[it], xg_send.at[it])
        wait_bytes(pp.at[it], sg_send.at[it])
        wait_bytes(qr.at[it], qr_send.at[it])

        wait_bytes(qr.at[it], qa_recv.at[it])
        q_now = jnp.dot(
            l_inverse,
            from_tiles(qg[it]),
            precision=HIGH,
            preferred_element_type=jnp.float32,
        )
        if it < ITERS - 1:
            qs[...] = right_factor(q_now)
        else:
            q_out[...] = q_now

    for it in range(ITERS):
        wait_bytes(qr.at[it], qa_send.at[it])


def finish(g, e, ph, q_ref, q_out, new_out, buffer, sem):
    copies = [pltpu.make_async_copy(q_ref, q_out, sem.at[2 * NZ])]
    copies[0].start()
    q_now = q_ref[...]
    high = q_now.astype(jnp.bfloat16)
    low = (q_now - high.astype(jnp.float32)).astype(jnp.bfloat16)
    right = jnp.concatenate([high, high, low, low], axis=0)
    for i in range(2 * NZ):
        rows = slice(i * ROWS, (i + 1) * ROWS)
        approx = jnp.dot(ph[rows, :], right, preferred_element_type=jnp.float32)
        merged = g[rows, :].astype(jnp.float32) + e[rows, :].astype(jnp.float32)
        buffer[rows, :] = (merged - approx).astype(jnp.bfloat16)
        copy = pltpu.make_async_copy(
            buffer.at[rows, :], new_out.at[0, rows, :], sem.at[i]
        )
        copy.start()
        copies.append(copy)
    for copy in copies:
        copy.wait()


def body(gradient, error, q_prev):
    f32, bf16 = jnp.float32, jnp.bfloat16
    dma = pltpu.SemaphoreType.DMA
    vmem = pl.BlockSpec(memory_space=pltpu.VMEM)
    hbm = pl.BlockSpec(memory_space=pltpu.HBM)
    q_t, g, e, p_hat = pl.pallas_call(
        kernel,
        out_shape=(
            jax.ShapeDtypeStruct((RANK, COLS), f32),
            jax.ShapeDtypeStruct((N, COLS), bf16),
            jax.ShapeDtypeStruct((N, COLS), bf16),
            jax.ShapeDtypeStruct((N, 4 * RANK), bf16),
        ),
        in_specs=[hbm, hbm, vmem],
        out_specs=(vmem, vmem, vmem, vmem),
        scratch_shapes=[
            pltpu.VMEM((COLS, 4 * RANK), bf16),
            pltpu.VMEM((ITERS, NZ, 16, 8, LANES), f32),
            pltpu.VMEM((ITERS, NZ, 16, 8, LANES), f32),
            pltpu.VMEM((ITERS, NZ, 16, 8, LANES), f32),
            pltpu.VMEM((ITERS, 3, NZ, 4, 8, LANES), f32),
            pltpu.VMEM((ITERS, NX, SKIPPED, 4, 8, LANES), f32),
            pltpu.VMEM((ITERS, NZ, 4, 8, LANES), f32),
            pltpu.VMEM((ITERS, N_DP - 1, 8, LANES), f32),
            pltpu.VMEM((ITERS, 2, NZ, 16, 8, LANES), f32),
            pltpu.VMEM((ITERS, N_DP, 8, LANES), f32),
            pltpu.VMEM((ITERS, N_DP - 1, 8, LANES), f32),
            pltpu.VMEM((ITERS, N_DP, 8, LANES), f32),
            pltpu.VMEM((RANK, 2 * RANK), f32),
            dma((NZ, 4)),
            dma((ITERS,)),
            dma((ITERS, N_SPANS)),
            dma((ITERS,)),
            dma((ITERS, N_SPANS)),
            dma((ITERS,)),
            dma((ITERS, N_SPANS)),
            dma((ITERS,)),
            dma((ITERS,)),
            dma((ITERS,)),
            dma((ITERS, N_SPANS)),
            dma((ITERS,)),
            dma((ITERS, N_SPANS)),
            dma((ITERS,)),
            dma((ITERS, N_SPANS)),
            dma((ITERS,)),
            dma((ITERS,)),
            dma((ITERS,)),
            dma((ITERS,)),
        ],
        compiler_params=pltpu.CompilerParams(
            collective_id=1, has_side_effects=True, vmem_limit_bytes=41 * 2**20
        ),
    )(gradient, error, q_prev.T)
    q_t, new_error = pl.pallas_call(
        finish,
        out_shape=(
            jax.ShapeDtypeStruct((RANK, COLS), f32),
            jax.ShapeDtypeStruct((1, N, COLS), bf16),
        ),
        in_specs=[vmem, vmem, vmem, vmem],
        out_specs=(
            pl.BlockSpec(memory_space=pl.ANY),
            pl.BlockSpec(memory_space=pl.ANY),
        ),
        scratch_shapes=[pltpu.VMEM((N, COLS), bf16), dma((2 * NZ + 1,))],
        compiler_params=pltpu.CompilerParams(vmem_limit_bytes=40 * 2**20),
    )(g, e, p_hat, q_t)
    return q_t.T, new_error


def solution(mesh):
    return jax.shard_map(
        body,
        mesh=mesh,
        in_specs=(P("dp", None, "tensor"), P("dp", None, "tensor"), P("tensor", None)),
        out_specs=(P("tensor", None), P("dp", None, "tensor")),
        check_vma=False,
    )
```

```python
import functools

import jax
import jax.numpy as jnp
from jax import lax
from jax.experimental import pallas as pl
from jax.experimental.pallas import tpu as pltpu
from jax.sharding import PartitionSpec as P

N = 4096
RANK = 64
ITERS = 2
NX, NY, NZ = 4, 4, 8
N_DP = NY * NZ
N_T = 2 * NX
COLS = N // N_T
LANES = 128
PIECES = 3
EARLY = 40
DIRECT = (0, 1, 2)
SKIP = (0, 1)
SKIPPED = 3
MESH = pl.DeviceIdType.MESH
HIGH = lax.Precision.HIGHEST
NT = (((1,), (1,)), ((), ()))


def ring_distance(step, size):
    return min(step % size, -step % size)


def distance(o):
    return ring_distance(o[0], NY) + ring_distance(o[1], NZ)


OFFSETS = sorted(
    [(du, dz) for du in range(NY) for dz in range(NZ) if du or dz],
    key=lambda o: -distance(o),
)
GATHER_ORDER = [o for o in OFFSETS if not o[1]] + [o for o in OFFSETS if o[1]]

SLOTS = (4, 3, 5, 2, 6, 1, 7, 0)
SPANS = ((0, 1), (1, 3), (3, 5), (5, 7), (7, 8))
N_SPANS = len(SPANS)
ROWS = N // (2 * NZ)


def slot_of(dz):
    return SLOTS.index(dz % NZ)


def span_of(dz):
    return N_SPANS - 1 - ring_distance(dz, NZ)


def pieces_of(value):
    out = []
    for _ in range(PIECES):
        piece = value.astype(jnp.bfloat16).astype(jnp.float32)
        out.append(piece)
        value = value - piece
    return out


def split(value):
    return jnp.concatenate([p.astype(jnp.bfloat16) for p in pieces_of(value)], axis=0)


def right_factor(q_t):
    high, mid, low = pieces_of(q_t)
    first = jnp.concatenate([high, mid], axis=0).T
    second = jnp.concatenate([low, jnp.zeros_like(low)], axis=0).T
    return jnp.concatenate([first, second], axis=1).astype(jnp.bfloat16)


def pack(value):
    both = value[:, :LANES] + value[:, LANES:]
    top, bottom = both[:LANES], both[LANES:]
    lower = lax.broadcasted_iota(jnp.int32, (LANES, LANES), 1) < RANK
    kept = jnp.where(lower, top, bottom)
    moved = pltpu.roll(jnp.where(lower, bottom, top), RANK, 1)
    return (kept + moved).reshape(16, 8, LANES)


def unpack_transposed(tiles):
    value = tiles.reshape(LANES, LANES).T
    return jnp.concatenate([value[:RANK], value[RANK:]], axis=1)


def fold(value):
    total = value[0:RANK]
    for i in range(1, PIECES):
        total = total + value[i * RANK : (i + 1) * RANK]
    return total


def to_tiles(value):
    parts = [
        value[:, l * LANES : (l + 1) * LANES].reshape(8, 8, LANES)
        for l in range(value.shape[1] // LANES)
    ]
    return jnp.concatenate(parts, axis=0)


def from_tiles(value):
    parts = [
        value[8 * l : 8 * l + 8].reshape(RANK, LANES)
        for l in range(value.shape[0] // 8)
    ]
    return jnp.concatenate(parts, axis=1)


def eliminate(work, first, last):
    lane = lax.broadcasted_iota(jnp.int32, (RANK, 2 * RANK), 1)
    row = lax.broadcasted_iota(jnp.int32, (RANK, 1), 0)
    lane1 = lax.broadcasted_iota(jnp.int32, (1, 2 * RANK), 1)

    def step(j, carry):
        a = work[...]
        pivot_row = work[pl.ds(j, 1), :]
        pivot = jnp.sum(jnp.where(lane1 == j, pivot_row, 0.0), axis=1, keepdims=True)
        column = jnp.sum(jnp.where(lane == j, a, 0.0), axis=1, keepdims=True)
        column = jnp.where(row > j, column, 0.0)
        work[...] = a - column * (pivot_row / pivot)
        return carry

    lax.fori_loop(first, last, step, 0)


def inverse_factor(work):
    a = work[...]
    lane = lax.broadcasted_iota(jnp.int32, (RANK, 2 * RANK), 1)
    row = lax.broadcasted_iota(jnp.int32, (RANK, 2 * RANK), 0)
    diagonal = jnp.sum(jnp.where(lane == row, a, 0.0), axis=1, keepdims=True)
    return a[:, RANK:] / jnp.sqrt(diagonal)


def kernel(
    g_hbm, e_hbm, q_ref, q_out, g, e, ph,
    qs, pp, sb, xs, xr, x2r, acc, yr, pg, ps, qp, qr, qg, work,
    load_sem, sib_send, sib_recv, x_send, x_recv, x2_send, x2_recv, y_send, y_recv,
    ag_send, ag_recv, xg_send, xg_recv, sg_send, sg_recv,
    qr_send, qr_recv, qa_send, qa_recv,
):
    dp = lax.axis_index("dp")
    t = lax.axis_index("tensor")
    y, z = lax.div(dp, NZ), lax.rem(dp, NZ)
    x, c = lax.div(t, 2), lax.rem(t, 2)
    sibling = (dp, t + 1 - 2 * c)

    def around(place, step, size):
        return lax.rem(place + step % size, size)

    xs_at = [around(x, d, NX) for d in range(NX)]
    ys_at = [around(y, d, NY) for d in range(NY)]
    zs_at = [around(z, d, NZ) for d in range(NZ)]

    odd = lax.rem(z, 2)
    odds = (odd, 1 - odd)

    def device(y_at, z_at, x_at):
        return (y_at * NZ + z_at, 2 * x_at + c)

    def either(k, even_case, odd_case):
        return even_case * (1 - odds[k]) + odd_case * odds[k]

    line_place = [[either(k, xs_at[d], ys_at[d]) for d in range(NX)] for k in (0, 1)]
    plane_place = [line_place[1], line_place[0]]
    line_device = [
        [device(either(k, y, ys_at[d]), z, either(k, xs_at[d], x)) for d in range(NX)]
        for k in (0, 1)
    ]

    line_other_core = [
        [(line_device[k][d][0], line_device[k][d][1] + 1 - 2 * c) for d in range(NX)]
        for k in (0, 1)
    ]

    def plane_device(k, du, dz):
        return device(either(k, ys_at[du], y), zs_at[dz], either(k, x, xs_at[du]))

    own_plane = {o: plane_device(0, *o) for o in OFFSETS}
    other_plane = {o: plane_device(1, *o) for o in OFFSETS}
    dp_peers = [device(ys_at[o[0]], zs_at[o[1]], x) for o in OFFSETS]

    everyone = []
    for o in OFFSETS:
        everyone.append(own_plane[o])
        if o[0]:
            everyone.append(other_plane[o])
    everyone.append(sibling)
    everyone += [line_other_core[k][d] for k in (0, 1) for d in (1, 2, 3)]

    barrier = pltpu.get_barrier_semaphore()
    for peer in everyone:
        pl.semaphore_signal(barrier, inc=1, device_id=peer, device_id_type=MESH)

    def rows_of(core, slot):
        start = (core * NZ + zs_at[SLOTS[slot]]) * ROWS
        return pl.ds(pl.multiple_of(start, ROWS), ROWS)

    loads = []
    for slot in range(NZ):
        copies = []
        for i, core in enumerate((1 - c, c)):
            rows = rows_of(core, slot)
            for k, (hbm, vmem) in enumerate(((g_hbm, g), (e_hbm, e))):
                copy = pltpu.make_async_copy(
                    hbm.at[0, rows, :], vmem.at[rows, :], load_sem.at[slot, 2 * i + k]
                )
                copy.start()
                copies.append(copy)
        loads.append(copies)

    qs[...] = right_factor(q_ref[...])

    def send(src, dst, send_sem, recv_sem, target):
        pltpu.make_async_remote_copy(
            src_ref=src,
            dst_ref=dst,
            send_sem=send_sem,
            recv_sem=recv_sem,
            device_id=target,
            device_id_type=MESH,
        ).start()

    def wait_bytes(ref, sem):
        pltpu.make_async_copy(ref, ref, sem).wait()

    scale = 1.0 / N_DP
    for it in range(ITERS):

        def p_rows(core, slot):
            rows = rows_of(core, slot)
            factor = qs[...]
            a = jnp.dot(g[rows, :], factor, preferred_element_type=jnp.float32)
            b = jnp.dot(e[rows, :], factor, preferred_element_type=jnp.float32)
            return pack(a + b)

        def for_sibling(span):
            for slot in range(*SPANS[span]):
                pp[it, slot] = p_rows(1 - c, slot)

        def for_own(span):
            for slot in range(*SPANS[span]):
                xs[it, slot] = p_rows(c, slot)

        def slots(span):
            return pl.ds(SPANS[span][0], SPANS[span][1] - SPANS[span][0])

        def to_sibling(span):
            if span in SKIP:
                return
            send(
                pp.at[it, slots(span)],
                sb.at[it, slots(span)],
                sib_send.at[it],
                sib_recv.at[it, span],
                sibling,
            )

        def to_line(span):
            k = span % 2
            if span in SKIP:
                for d in (2, 1, 3, 0):
                    send(
                        pp.at[it, slots(span), pl.ds(4 * line_place[k][d], 4)],
                        x2r.at[it, d, slots(span)],
                        x2_send.at[it],
                        x2_recv.at[it, span],
                        line_other_core[k][d],
                    )
            else:
                wait_bytes(sb.at[it, slots(span)], sib_recv.at[it, span])
                for slot in range(*SPANS[span]):
                    xs[it, slot] = xs[it, slot] + sb[it, slot]
            for d in (2, 1, 3):
                send(
                    xs.at[it, slots(span), pl.ds(4 * line_place[k][d], 4)],
                    xr.at[it, d - 1, slots(span)],
                    x_send.at[it],
                    x_recv.at[it, span],
                    line_device[k][d],
                )

        def to_plane(span):
            wait_bytes(xr.at[it, :, slots(span)], x_recv.at[it, span])
            if span in SKIP:
                wait_bytes(x2r.at[it, :, slots(span)], x2_recv.at[it, span])
            k = span % 2
            for slot in range(*SPANS[span]):
                total = xs[it, slot, pl.ds(4 * line_place[k][0], 4)]
                for d in (1, 2, 3):
                    total = total + xr[it, d - 1, slot]
                if span in SKIP:
                    for d in range(NX):
                        total = total + x2r[it, d, slot]
                acc[it, slot] = total * scale
            for du in (2, 1, 3, 0):
                for slot in range(*SPANS[span]):
                    o = (du, SLOTS[slot])
                    if o == (0, 0):
                        continue
                    send(
                        acc.at[it, slot, plane_place[k][du]],
                        yr.at[it, OFFSETS.index(o)],
                        y_send.at[it],
                        y_recv.at[it],
                        (own_plane, other_plane)[k][o],
                    )

        if it == 0:
            for span in range(N_SPANS):
                for slot in range(*SPANS[span]):
                    for copy in loads[slot]:
                        copy.wait()
                for_sibling(span)
                for_own(span)
            pl.semaphore_wait(barrier, len(everyone))
            for span in range(N_SPANS):
                to_sibling(span)
            for span in range(N_SPANS):
                to_line(span)
        else:
            for span in SKIP:
                for_sibling(span)
                for_own(span)
                to_line(span)
            rest = [span for span in range(N_SPANS) if span not in SKIP]
            for span in rest:
                for_sibling(span)
                to_sibling(span)
            for i, span in enumerate(rest):
                for_own(span)
                if i:
                    to_line(rest[i - 1])
            to_line(rest[-1])
        for span in range(N_SPANS):
            to_plane(span)

        near = slot_of(0)
        mine = 4 * line_place[0][0] + plane_place[0][0]
        own = acc[it, near, plane_place[0][0]]
        wait_bytes(yr.at[it], y_recv.at[it])
        pg[it, c, near, mine] = own + jnp.sum(yr[it], axis=0)

        for o in GATHER_ORDER:
            send(
                pg.at[it, c, near, mine],
                pg.at[it, c, slot_of(-o[1]), mine],
                ag_send.at[it],
                ag_recv.at[it, span_of(o[1])],
                own_plane[o],
            )

        for span in range(N_SPANS - 1, -1, -1):
            k = span % 2
            tiles = pg.at[it, c, slots(span), pl.ds(4 * line_place[k][0], 4)]
            if span == N_SPANS - 1:
                wait_bytes(yr.at[it, pl.ds(0, 3)], ag_recv.at[it, span])
            else:
                wait_bytes(tiles, ag_recv.at[it, span])
            for d in (2, 1, 3):
                send(
                    tiles, tiles, xg_send.at[it], xg_recv.at[it, span], line_device[k][d]
                )
            if span in DIRECT:
                for target in [line_other_core[k][d] for d in (2, 1, 3)] + [sibling]:
                    send(tiles, tiles, sg_send.at[it], sg_recv.at[it, span], target)

        q_acc = jnp.zeros((RANK, COLS), jnp.float32)

        def q_rows(core, place, span, q_acc):
            for slot in range(*SPANS[span]):
                rows = rows_of(core, slot)
                lhs = split(unpack_transposed(pg[it, core, slot]))
                start = (place * NZ + slot) * ROWS
                ps[:, start : start + ROWS] = lhs
                a = jnp.dot(lhs, g[rows, :], preferred_element_type=jnp.float32)
                b = jnp.dot(lhs, e[rows, :], preferred_element_type=jnp.float32)
                q_acc = q_acc + fold(a + b)
            return q_acc

        for span in range(N_SPANS - 1, -1, -1):
            wait_bytes(xr.at[it, :, slots(span)], xg_recv.at[it, span])
            if span not in DIRECT:
                chunk = pg.at[it, c, slots(span)]
                send(chunk, chunk, sg_send.at[it], sg_recv.at[it, span], sibling)
            q_acc = q_rows(c, 0, span, q_acc)
        for span in range(N_SPANS - 1, -1, -1):
            wait_bytes(pg.at[it, 1 - c, slots(span)], sg_recv.at[it, span])
            q_acc = q_rows(1 - c, 1, span, q_acc)

        qp[it] = to_tiles(q_acc * scale)
        for k, peer in enumerate(dp_peers):
            send(
                qp.at[it, peer[0]],
                qr.at[it, k],
                qr_send.at[it],
                qr_recv.at[it],
                peer,
            )

        gram = lax.dot_general(
            ps[...], ps[...], NT, preferred_element_type=jnp.float32
        )
        square = jnp.zeros((RANK, RANK), jnp.float32)
        for i in range(PIECES):
            for j in range(PIECES):
                square = square + gram[
                    i * RANK : (i + 1) * RANK, j * RANK : (j + 1) * RANK
                ]
        row = lax.broadcasted_iota(jnp.int32, (RANK, RANK), 0)
        lane = lax.broadcasted_iota(jnp.int32, (RANK, RANK), 1)
        eye = jnp.where(row == lane, 1.0, 0.0)
        work[...] = jnp.concatenate([square, eye], axis=1)
        eliminate(work, 0, EARLY)

        wait_bytes(qr.at[it], qr_recv.at[it])
        qg[it, dp] = qp[it, dp] + jnp.sum(qr[it], axis=0)
        for peer in dp_peers:
            send(
                qg.at[it, dp],
                qg.at[it, dp],
                qa_send.at[it],
                qa_recv.at[it],
                peer,
            )
        eliminate(work, EARLY, RANK)
        l_inverse = inverse_factor(work)

        if it == ITERS - 1:
            none = jnp.zeros((RANK, RANK), jnp.float32)
            twice = jnp.concatenate(
                [
                    jnp.concatenate([l_inverse, none], axis=1),
                    jnp.concatenate([none, l_inverse], axis=1),
                ],
                axis=0,
            )
            lower = lax.broadcasted_iota(jnp.int32, (LANES, LANES), 1) < RANK
            for i in range(2 * NZ):
                hat = lax.dot_general(
                    pg[it, i // NZ, i % NZ].reshape(LANES, LANES),
                    twice,
                    NT,
                    precision=HIGH,
                    preferred_element_type=jnp.float32,
                )
                high = hat.astype(jnp.bfloat16).astype(jnp.float32)
                low = hat - high
                top = jnp.where(lower, high, pltpu.roll(low, RANK, 1))
                bottom = jnp.where(lower, pltpu.roll(high, RANK, 1), low)
                both = jnp.concatenate([top, bottom], axis=0).astype(jnp.bfloat16)
                ph[rows_of(i // NZ, i % NZ), :] = jnp.concatenate([both, both], axis=1)

        wait_bytes(pp.at[it, pl.ds(SKIPPED, NZ - SKIPPED)], sib_send.at[it])
        wait_bytes(x2r.at[it], x2_send.at[it])
        wait_bytes(xr.at[it], x_send.at[it])
        wait_bytes(yr.at[it], y_send.at[it])
        wait_bytes(yr.at[it], ag_send.at[it])
        wait_bytes(xr.at[it], xg_send.at[it])
        wait_bytes(pp.at[it], sg_send.at[it])
        wait_bytes(qr.at[it], qr_send.at[it])

        wait_bytes(qr.at[it], qa_recv.at[it])
        q_now = jnp.dot(
            l_inverse,
            from_tiles(qg[it]),
            precision=HIGH,
            preferred_element_type=jnp.float32,
        )
        if it < ITERS - 1:
            qs[...] = right_factor(q_now)
        else:
            q_out[...] = q_now

    for it in range(ITERS):
        wait_bytes(qr.at[it], qa_send.at[it])


def finish(g, e, ph, q_ref, q_out, new_out, buffer, sem):
    copies = [pltpu.make_async_copy(q_ref, q_out, sem.at[2 * NZ])]
    copies[0].start()
    q_now = q_ref[...]
    high = q_now.astype(jnp.bfloat16)
    low = (q_now - high.astype(jnp.float32)).astype(jnp.bfloat16)
    right = jnp.concatenate([high, high, low, low], axis=0)
    for i in range(2 * NZ):
        rows = slice(i * ROWS, (i + 1) * ROWS)
        approx = jnp.dot(ph[rows, :], right, preferred_element_type=jnp.float32)
        merged = g[rows, :].astype(jnp.float32) + e[rows, :].astype(jnp.float32)
        buffer[rows, :] = (merged - approx).astype(jnp.bfloat16)
        copy = pltpu.make_async_copy(
            buffer.at[rows, :], new_out.at[0, rows, :], sem.at[i]
        )
        copy.start()
        copies.append(copy)
    for copy in copies:
        copy.wait()


def body(gradient, error, q_prev):
    f32, bf16 = jnp.float32, jnp.bfloat16
    dma = pltpu.SemaphoreType.DMA
    vmem = pl.BlockSpec(memory_space=pltpu.VMEM)
    hbm = pl.BlockSpec(memory_space=pltpu.HBM)
    q_t, g, e, p_hat = pl.pallas_call(
        kernel,
        out_shape=(
            jax.ShapeDtypeStruct((RANK, COLS), f32),
            jax.ShapeDtypeStruct((N, COLS), bf16),
            jax.ShapeDtypeStruct((N, COLS), bf16),
            jax.ShapeDtypeStruct((N, 4 * RANK), bf16),
        ),
        in_specs=[hbm, hbm, vmem],
        out_specs=(vmem, vmem, vmem, vmem),
        scratch_shapes=[
            pltpu.VMEM((COLS, 4 * RANK), bf16),
            pltpu.VMEM((ITERS, NZ, 16, 8, LANES), f32),
            pltpu.VMEM((ITERS, NZ, 16, 8, LANES), f32),
            pltpu.VMEM((ITERS, NZ, 16, 8, LANES), f32),
            pltpu.VMEM((ITERS, 3, NZ, 4, 8, LANES), f32),
            pltpu.VMEM((ITERS, NX, SKIPPED, 4, 8, LANES), f32),
            pltpu.VMEM((ITERS, NZ, 4, 8, LANES), f32),
            pltpu.VMEM((ITERS, N_DP - 1, 8, LANES), f32),
            pltpu.VMEM((ITERS, 2, NZ, 16, 8, LANES), f32),
            pltpu.VMEM((PIECES * RANK, N), bf16),
            pltpu.VMEM((ITERS, N_DP, 8, LANES), f32),
            pltpu.VMEM((ITERS, N_DP - 1, 8, LANES), f32),
            pltpu.VMEM((ITERS, N_DP, 8, LANES), f32),
            pltpu.VMEM((RANK, 2 * RANK), f32),
            dma((NZ, 4)),
            dma((ITERS,)),
            dma((ITERS, N_SPANS)),
            dma((ITERS,)),
            dma((ITERS, N_SPANS)),
            dma((ITERS,)),
            dma((ITERS, N_SPANS)),
            dma((ITERS,)),
            dma((ITERS,)),
            dma((ITERS,)),
            dma((ITERS, N_SPANS)),
            dma((ITERS,)),
            dma((ITERS, N_SPANS)),
            dma((ITERS,)),
            dma((ITERS, N_SPANS)),
            dma((ITERS,)),
            dma((ITERS,)),
            dma((ITERS,)),
            dma((ITERS,)),
        ],
        compiler_params=pltpu.CompilerParams(
            collective_id=1, has_side_effects=True, vmem_limit_bytes=41 * 2**20
        ),
    )(gradient, error, q_prev.T)
    q_t, new_error = pl.pallas_call(
        finish,
        out_shape=(
            jax.ShapeDtypeStruct((RANK, COLS), f32),
            jax.ShapeDtypeStruct((1, N, COLS), bf16),
        ),
        in_specs=[vmem, vmem, vmem, vmem],
        out_specs=(
            pl.BlockSpec(memory_space=pl.ANY),
            pl.BlockSpec(memory_space=pl.ANY),
        ),
        scratch_shapes=[pltpu.VMEM((N, COLS), bf16), dma((2 * NZ + 1,))],
        compiler_params=pltpu.CompilerParams(vmem_limit_bytes=40 * 2**20),
    )(g, e, p_hat, q_t)
    return q_t.T, new_error


def solution(mesh):
    return jax.shard_map(
        body,
        mesh=mesh,
        in_specs=(P("dp", None, "tensor"), P("dp", None, "tensor"), P("tensor", None)),
        out_specs=(P("tensor", None), P("dp", None, "tensor")),
        check_vma=False,
    )
```
